512 devices in a mesh: dp: 32 (over y_hi, x, core), axial: 16 (over z, y_lo).
Axes of the slice: x: 4, y: 8 (y_hi: 4, y_lo: 2; y = y_hi * 2 + y_lo), z: 8, core: 2. Of those that a mesh axis runs over, the one named last changes fastest.
Arguments:
- normed_homolog_features: bfloat16 [32, 128, 128, 256], P('dp', None, 'axial'), may hold values from -6 to 6
- first_factor_matrix: bfloat16 [256, 32], replicated, may hold values from -0.375 to 0.375
- second_factor_matrix: bfloat16 [256, 32], replicated, may hold values from -0.375 to 0.375
- output_weight: bfloat16 [1024, 128], replicated, may hold values from -2 to 2
- pair_update_gradient: float32 [32, 128, 128, 128], P('dp', 'axial'), may hold values from -6 to 6
Outputs:
- pair_update: float32 [32, 128, 128, 128], P('dp', 'axial')
- grad_msa: bfloat16 [32, 128, 128, 256], P('dp', None, 'axial')
- grad_left: float32 [256, 32], replicated
- grad_right: float32 [256, 32], replicated
- grad_out: float32 [1024, 128], replicated
The draws below stay inside these ranges and needn't reach their ends.
All inputs are finite; a program needn't handle non-finite values.
Results may differ from the reference program's by a relative error of at most 0.007.
Values may be sent and summed in bfloat16 or wider, within the bound.
No kernel may reach another device: no remote copies, remote signals or barrier semaphores. Data moves between devices by JAX's collectives and lax.ppermute only.
A program may use at most 64 MiB of HBM per device.

```python
import jax
import jax.numpy as jnp
from jax import lax

FEATURE_DIM = 256
HIDDEN_FACTORS = 32
CZ = 128
HOMOLOG_NUMBER = 128
CHAIN_LENGTH = 128
BATCH_EXAMPLES = 32


def raised(values, rng, source, target, shards_of, factor):
    def block_of(position):
        return (jnp.arange(values.shape[position]) // (values.shape[position] // shards_of)).reshape((-1,) + (1,) * (values.ndim - 1 - position))

    near = jax.random.permutation(rng, shards_of)[block_of(target)]
    far = (block_of(target) + shards_of // 2) % shards_of
    return jnp.where((block_of(source) == near) | (block_of(source) == far), factor * values, values)


def shard_levels(stream_key, dims, shards, smallest, high):
    def one(dim, shards_of):
        draws = jax.random.uniform(jax.random.fold_in(jax.random.fold_in(stream_key, 6), dim), (shards_of,), jnp.float32, smallest / len(shards), high / len(shards))
        return jnp.repeat(jnp.exp(draws), dims[dim] // shards_of).reshape((-1,) + (1,) * (len(dims) - dim - 1))

    loudness = one(*shards[0])
    for cut in shards[1:]:
        loudness = loudness * one(*cut)
    return loudness


def centred(stream_key, dims, scale, bound, pieces=(), dtype=jnp.bfloat16):
    gain = shard_levels(stream_key, dims, pieces, -0.22, 0.18) if pieces else 1.0
    drawn = jax.random.normal(stream_key, dims, jnp.float32) * scale * gain
    return jnp.minimum(jnp.maximum(drawn, -bound), bound).astype(dtype)


def gaussian_with(own_key, dims, scale, reach, shards, heavy, kind=jnp.bfloat16):
    drawn = scale * jax.random.normal(own_key, dims, jnp.float32)
    if shards:
        drawn = drawn * shard_levels(own_key, dims, shards, -0.22, 0.18)
    return jnp.clip(raised(drawn, jax.random.fold_in(own_key, 3), *heavy), -reach, reach).astype(kind)


def setup_inputs(seed: int = 0) -> dict:
    keys = jax.random.split(jax.random.key(seed), 6)
    return {
        "normed_homolog_features": centred(keys[0], (BATCH_EXAMPLES, HOMOLOG_NUMBER, CHAIN_LENGTH, FEATURE_DIM), 1.0, 6.0, ((0, 32), (2, 16))),
        "first_factor_matrix": centred(keys[1], (FEATURE_DIM, HIDDEN_FACTORS), FEATURE_DIM ** -0.5, 0.375),
        "second_factor_matrix": centred(keys[2], (FEATURE_DIM, HIDDEN_FACTORS), FEATURE_DIM ** -0.5, 0.375),
        "output_weight": centred(keys[3], (HIDDEN_FACTORS * HIDDEN_FACTORS, CZ), (HIDDEN_FACTORS * HIDDEN_FACTORS // HOMOLOG_NUMBER) ** -0.5, 2.0),
        "pair_update_gradient": gaussian_with(keys[4], (BATCH_EXAMPLES, CHAIN_LENGTH, CHAIN_LENGTH, CZ), 1.0, 6.0, ((0, 32), (1, 16)), (1, 2, 16, 2.0), jnp.float32),
    }


def reference(normed_homolog_features, first_factor_matrix, second_factor_matrix, output_weight, pair_update_gradient):
    def crop_function(inputs):
        example_homolog_entries, cotangent = inputs
        homolog_matrix_merged = example_homolog_entries.reshape(HOMOLOG_NUMBER * CHAIN_LENGTH, FEATURE_DIM)
        left_projected = jnp.dot(homolog_matrix_merged, first_factor_matrix, preferred_element_type=jnp.float32).astype(jnp.bfloat16).reshape(HOMOLOG_NUMBER, CHAIN_LENGTH, HIDDEN_FACTORS)
        right_projected = jnp.dot(homolog_matrix_merged, second_factor_matrix, preferred_element_type=jnp.float32).astype(jnp.bfloat16).reshape(HOMOLOG_NUMBER, CHAIN_LENGTH, HIDDEN_FACTORS)
        outer = (jnp.einsum('sic,sje->ijce', left_projected.astype(jnp.float32), right_projected.astype(jnp.float32)) / HOMOLOG_NUMBER).astype(jnp.bfloat16).reshape(CHAIN_LENGTH * CHAIN_LENGTH, HIDDEN_FACTORS * HIDDEN_FACTORS)
        pair_delta = jnp.dot(outer, output_weight, preferred_element_type=jnp.float32).reshape(CHAIN_LENGTH, CHAIN_LENGTH, CZ)
        grad_pair = cotangent.astype(jnp.bfloat16).reshape(CHAIN_LENGTH * CHAIN_LENGTH, CZ)
        output_weight_gradient = jnp.dot(outer.T, grad_pair, preferred_element_type=jnp.float32)
        grad_outer = jnp.dot(grad_pair, output_weight.T, preferred_element_type=jnp.float32).astype(jnp.bfloat16).reshape(CHAIN_LENGTH, CHAIN_LENGTH, HIDDEN_FACTORS, HIDDEN_FACTORS)
        first_factor_cotangent = (jnp.einsum('ijce,sje->sic', grad_outer.astype(jnp.float32), right_projected.astype(jnp.float32)) / HOMOLOG_NUMBER).astype(jnp.bfloat16).reshape(HOMOLOG_NUMBER * CHAIN_LENGTH, HIDDEN_FACTORS)
        second_factor_cotangent = (jnp.einsum('ijce,sic->sje', grad_outer.astype(jnp.float32), left_projected.astype(jnp.float32)) / HOMOLOG_NUMBER).astype(jnp.bfloat16).reshape(HOMOLOG_NUMBER * CHAIN_LENGTH, HIDDEN_FACTORS)
        homolog_cotangent_entries = (jnp.dot(first_factor_cotangent, first_factor_matrix.T, preferred_element_type=jnp.float32) + jnp.dot(second_factor_cotangent, second_factor_matrix.T, preferred_element_type=jnp.float32)).astype(jnp.bfloat16).reshape(HOMOLOG_NUMBER, CHAIN_LENGTH, FEATURE_DIM)
        left_weight_gradient = jnp.dot(homolog_matrix_merged.T, first_factor_cotangent, preferred_element_type=jnp.float32)
        right_weight_gradient = jnp.dot(homolog_matrix_merged.T, second_factor_cotangent, preferred_element_type=jnp.float32)
        return pair_delta, homolog_cotangent_entries, left_weight_gradient, right_weight_gradient, output_weight_gradient

    pair_delta, homolog_cotangent_entries, left_weight_gradient, right_weight_gradient, output_weight_gradient = lax.map(crop_function, (normed_homolog_features, pair_update_gradient))
    return (pair_delta, homolog_cotangent_entries, jnp.sum(left_weight_gradient, axis=0) / BATCH_EXAMPLES, jnp.sum(right_weight_gradient, axis=0) / BATCH_EXAMPLES, jnp.sum(output_weight_gradient, axis=0) / BATCH_EXAMPLES)
```

```python
import jax
import jax.numpy as jnp
from jax import lax
from jax.experimental import pallas as pl
from jax.experimental.pallas import tpu as pltpu
from jax.sharding import Mesh, PartitionSpec as P

BF16 = jnp.bfloat16
F32 = jnp.float32
ROW = ("zl", "yl")
COL = "zh"
XC = ("x", "core")
YH = "yh"
AXIAL = ("zh", "zl", "yl")
DP = ("yh", "x", "core")

S = 128
RES = 8
C = 32
Z = 128
F = 256
G = 4


def dot(a, b, dims):
    return lax.dot_general(a, b, (dims, ((), ())), preferred_element_type=F32)


def nn(a, b):
    return dot(a, b, ((1,), (0,)))


def nt(a, b):
    return dot(a, b, ((1,), (1,)))


def tn(a, b):
    return dot(a, b, ((0,), (0,)))


def call(kernel, out, *args, scratch=(), flops=0):
    size = sum(a.size * a.dtype.itemsize for a in args) + sum(
        o.size * o.dtype.itemsize for o in out
    )
    return pl.pallas_call(
        kernel,
        out_shape=out,
        in_specs=[pl.BlockSpec(memory_space=pltpu.VMEM)] * len(args),
        out_specs=[pl.BlockSpec(memory_space=pltpu.VMEM)] * len(out),
        scratch_shapes=list(scratch),
        compiler_params=pltpu.CompilerParams(vmem_limit_bytes=48 * 1024 * 1024),
        cost_estimate=pl.CostEstimate(flops=flops, bytes_accessed=size, transcendentals=0),
    )(*args)


def shape(dims, dtype):
    return jax.ShapeDtypeStruct(dims, dtype)


def exchange(x, axes):
    return lax.all_to_all(x, axes, split_axis=0, concat_axis=0, tiled=True)


def channel_major():
    n = RES * C
    p = lax.broadcasted_iota(jnp.int32, (n, n), 0)
    q = lax.broadcasted_iota(jnp.int32, (n, n), 1)
    same = ((p >> 3) == (q & 31)) & ((p & 7) == (q >> 5))
    return jnp.where(same, 1.0, 0.0).astype(BF16)


def project_kernel(x_ref, f1_ref, f2_ref, cot_ref, row_ref, col_ref):
    for b in range(G):
        for i in range(RES):
            for h in range(2):
                at = i * 128 + h * 64 + b * 8
                pair = jnp.concatenate([cot_ref[at : at + 8, :], cot_ref[at + 32 : at + 40, :]], axis=0)
                row_ref[b, i * 32 + h * 16 : i * 32 + h * 16 + 16, :] = pair.astype(BF16)
    factors = jnp.concatenate([f1_ref[...].astype(F32).T, f2_ref[...].astype(F32).T], axis=0).astype(BF16)
    left, right = [], []
    for i in range(RES):
        both = nt(factors, x_ref[i]).astype(BF16)
        left.append(both[:C])
        right.append(both[C:])
    left = jnp.concatenate(left, axis=0)
    right = nn(channel_major(), jnp.concatenate(right, axis=0)).astype(BF16)
    for b in range(G):
        row_ref[b, 256:512, :] = left
        col_ref[b] = right


def swap_to_channels(o):
    blocks = []
    for e in range(C):
        at = e * 32
        blocks.append(
            jnp.concatenate([o[i * 32 : i * 32 + 32, at : at + 32] for i in range(4)], axis=1)
        )
    return jnp.concatenate(blocks, axis=0)


def swap_to_residues(g):
    rows = []
    for i in range(4):
        rows.append(
            jnp.concatenate(
                [g[e * 32 : e * 32 + 32, i * 32 : i * 32 + 32] for e in range(C)], axis=1
            )
        )
    return jnp.concatenate(rows, axis=0)


def main_kernel(row_ref, col_ref, w_ref, out_ref, rg_ref, wide, gout, grads):
    wide[...] = w_ref[...].astype(F32)
    weight = jnp.concatenate([wide[pl.ds(e, 32, stride=32), :] for e in range(C)], axis=0)
    weight_t = weight.T.astype(BF16)
    weight = weight.astype(BF16)
    right = jnp.concatenate(
        [col_ref[a].astype(F32).reshape(C, RES, S) for a in range(G)], axis=1
    ).reshape(C * G * RES, S).astype(BF16)
    for q in range(8):
        b, at = q // 2, (q % 2) * 128
        left = row_ref[b, 256 + at : 256 + at + 128, :]
        cot = row_ref[b, at : at + 128, :]
        outer = swap_to_channels((nt(left, right) * (1.0 / S)).astype(BF16))
        out_ref[b, at : at + 128, :] = nn(weight_t, outer).T.astype(BF16)
        term = nn(outer, cot)
        if q == 0:
            gout[...] = term
        else:
            gout[...] += term
        grad = swap_to_residues(nt(weight, cot).astype(BF16))
        grads[q * 128 : q * 128 + 128, :] = grad
        out_ref[b, 256 + at : 256 + at + 128, :] = (nn(grad, right) * (1.0 / S)).astype(BF16)
    for b in range(G):
        out_ref[b, 512:768, :] = gout[b * 256 : b * 256 + 256, :].astype(BF16)
    lefts = jnp.concatenate([row_ref[b, 256:512, :] for b in range(G)], axis=0)
    rg = (tn(lefts, grads[...]) * (1.0 / S)).T.reshape(C, G, RES, S)
    for a in range(G):
        rg_ref[a] = rg[:, a].reshape(C * RES, S).astype(BF16)


def merge_kernel(back_ref, rg_ref, col_ref):
    total = sum(back_ref[b, 512:768, :].astype(F32) for b in range(G)).astype(BF16)
    for a in range(G):
        col_ref[a, 0:256, :] = rg_ref[a]
        col_ref[a, 256:320, :] = total[a * 64 : a * 64 + 64]


def update_kernel(back_ref, out_ref):
    for b in range(G):
        part = back_ref[b, 0:256, :].astype(F32)
        for i in range(RES):
            for a in range(G):
                at = i * 128 + a * 32 + b * 8
                out_ref[at : at + 8, :] = part[i * 32 + a * 8 : i * 32 + a * 8 + 8, :]


def factor_kernel(back_ref, col_ref, x_ref, grad_ref, tail_ref):
    left = sum(back_ref[b, 256:512, :].astype(F32) for b in range(G)).astype(BF16)
    right = sum(col_ref[a, 0:256, :].astype(F32) for a in range(G)).astype(BF16)
    right = tn(channel_major(), right).astype(BF16)
    total = jnp.zeros((2 * C, F), F32)
    for i in range(RES):
        both = jnp.concatenate([left[i * C : i * C + C], right[i * C : i * C + C]], axis=0)
        grad_ref[i] = both
        total = total + nn(both, x_ref[i])
    gout = sum(col_ref[a, 256:320, :].astype(F32) for a in range(G))
    for k in range(8):
        half, at = k // 4, (k % 4) * 16
        tail_ref[k, 0:16, :] = total[at : at + 16, half * 128 : half * 128 + 128]
        tail_ref[k, 16:24, :] = gout[k * 8 : k * 8 + 8]


def msa_kernel(grad_ref, f1_ref, f2_ref, out_ref):
    factors = jnp.concatenate([f1_ref[...].astype(F32).T, f2_ref[...].astype(F32).T], axis=0).astype(BF16)
    for i in range(RES):
        out_ref[i] = tn(grad_ref[i], factors).astype(BF16)


def sum_kernel(in_ref, out_ref):
    total = in_ref[0]
    for k in range(1, in_ref.shape[0]):
        total = total + in_ref[k]
    for k in range(out_ref.shape[0]):
        out_ref[k] = total


def gather_kernel(in_ref, out_ref):
    total = in_ref[0, 0:16, :]
    for k in range(1, 16):
        total = total + in_ref[k, 0:16, :]
    total = total.astype(BF16)
    gout = jnp.concatenate([in_ref[k, 16:24, :] for k in range(16)], axis=0).astype(BF16)
    for k in range(8):
        out_ref[k, 0:16, :] = total
        out_ref[k, 16:144, :] = gout


def final_kernel(in_ref, gl_ref, gr_ref, gout_ref, wide):
    scale = 1.0 / 32
    halves = [
        jnp.concatenate([in_ref[h * 4 + k, 0:16, :].astype(F32) for k in range(4)], axis=0)
        for h in range(2)
    ]
    both = jnp.concatenate(halves, axis=1).T * scale
    gl_ref[...] = both[:, 0:C]
    gr_ref[...] = both[:, C : 2 * C]
    for k in range(8):
        part = in_ref[k, 16:144, :].astype(F32) * scale
        for a in range(G):
            for b in range(G):
                at = b * 256 + a * 64 + k * 8
                wide[at : at + 8, :] = part[(a * 4 + b) * 8 : (a * 4 + b) * 8 + 8]
    for c in range(C):
        gout_ref[c * 32 : c * 32 + 32, :] = wide[pl.ds(c, 32, stride=32), :]


def per_device(x, f1, f2, w, cot):
    x = x[0].transpose(1, 0, 2)
    cot = cot[0].reshape(RES * 128, Z)
    row, col = call(
        project_kernel, [shape((G, 512, S), BF16), shape((G, 256, S), BF16)], x, f1, f2, cot, flops=33554432
    )
    row = exchange(row, ROW)
    col = exchange(col, COL)
    back, rg = call(
        main_kernel,
        [shape((G, 768, 128), BF16), shape((G, 256, S), BF16)],
        row,
        col,
        w,
        scratch=[pltpu.VMEM((1024, 128), F32), pltpu.VMEM((1024, 128), F32), pltpu.VMEM((1024, 1024), BF16)],
        flops=6 * 2 * 1024 * 1024 * 128,
    )
    back = exchange(back, ROW)
    (col,) = call(merge_kernel, [shape((G, 320, 128), BF16)], back, rg)
    col = exchange(col, COL)
    (update,) = call(update_kernel, [shape((RES * 128, Z), F32)], back)
    grad, tail = call(
        factor_kernel, [shape((RES, 2 * C, S), BF16), shape((8, 24, 128), F32)], back, col, x, flops=33554432
    )
    (msa,) = call(msa_kernel, [shape((RES, S, F), BF16)], grad, f1, f2, flops=33554432)
    tail = exchange(tail, XC)
    (tail,) = call(sum_kernel, [shape((G, 24, 128), F32)], tail)
    tail = exchange(tail, YH)
    (tail,) = call(sum_kernel, [shape((16, 24, 128), F32)], tail)
    tail = exchange(tail, AXIAL)
    (tail,) = call(gather_kernel, [shape((8, 144, 128), BF16)], tail)
    tail = exchange(tail, XC)
    gl, gr, gout = call(
        final_kernel,
        [shape((F, C), F32), shape((F, C), F32), shape((1024, 128), F32)],
        tail,
        scratch=[pltpu.VMEM((1024, 128), F32)],
    )
    return update.reshape(1, RES, 128, Z), msa.transpose(1, 0, 2)[None], gl, gr, gout


def solution(mesh):
    split = Mesh(mesh.devices.reshape(4, 4, 2, 4, 2, 2), ("yh", "x", "core", "zh", "zl", "yl"))
    in_specs = (P(DP, None, AXIAL, None), P(), P(), P(), P(DP, AXIAL, None, None))
    out_specs = (P(DP, AXIAL, None, None), P(DP, None, AXIAL, None), P(), P(), P())
    return jax.shard_map(per_device, mesh=split, in_specs=in_specs, out_specs=out_specs, check_vma=False)
```

```python
import jax
import jax.numpy as jnp
from jax import lax
from jax.experimental import pallas as pl
from jax.experimental.pallas import tpu as pltpu
from jax.sharding import Mesh, PartitionSpec as P

BF16 = jnp.bfloat16
F32 = jnp.float32
ROW = ("zl", "yl")
COL = "zh"
NEAR = ("x", "core", "zl", "yl")
FAR = ("yh", "zh")
AXIAL = ("zh", "zl", "yl")
DP = ("yh", "x", "core")

S = 128
RES = 8
C = 32
Z = 128
F = 256
G = 4


def dot(a, b, dims):
    return lax.dot_general(a, b, (dims, ((), ())), preferred_element_type=F32)


def nn(a, b):
    return dot(a, b, ((1,), (0,)))


def nt(a, b):
    return dot(a, b, ((1,), (1,)))


def tn(a, b):
    return dot(a, b, ((0,), (0,)))


def call(kernel, out, *args, scratch=(), flops=0, hbm=False, limit=96):
    size = sum(a.size * a.dtype.itemsize for a in args) + sum(
        o.size * o.dtype.itemsize for o in out
    )
    return pl.pallas_call(
        kernel,
        out_shape=out,
        in_specs=[pl.BlockSpec(memory_space=pltpu.HBM if hbm else pltpu.VMEM)] * len(args),
        out_specs=[pl.BlockSpec(memory_space=pltpu.VMEM)] * len(out),
        scratch_shapes=list(scratch),
        compiler_params=pltpu.CompilerParams(vmem_limit_bytes=limit * 1024 * 256),
        cost_estimate=pl.CostEstimate(flops=flops, bytes_accessed=size, transcendentals=0),
    )(*args)


def shape(dims, dtype):
    return jax.ShapeDtypeStruct(dims, dtype)


def exchange(x, axes):
    return lax.all_to_all(x, axes, split_axis=0, concat_axis=0, tiled=True)


def channel_major():
    n = RES * C
    p = lax.broadcasted_iota(jnp.int32, (n, n), 0)
    q = lax.broadcasted_iota(jnp.int32, (n, n), 1)
    same = ((p >> 3) == (q & 31)) & ((p & 7) == (q >> 5))
    return jnp.where(same, 1.0, 0.0).astype(BF16)


def project_kernel(x_hbm, f_hbm, cot_hbm, row_ref, right_ref, xt_ref, x_ref, f_ref, cot_ref, wide, sems):
    copies = [
        pltpu.make_async_copy(f_hbm, f_ref, sems.at[0]),
        pltpu.make_async_copy(x_hbm, x_ref, sems.at[1]),
        pltpu.make_async_copy(cot_hbm, cot_ref, sems.at[2]),
    ]
    for copy in copies:
        copy.start()
    for copy in copies[:2]:
        copy.wait()
    factors = f_ref[...]
    for h in range(2):
        wide[h] = x_ref[:, h * 128 : h * 128 + 128].astype(F32)
    left, right = [], []
    for i in range(RES):
        x = jnp.concatenate([wide[h, pl.ds(i, S, stride=RES), :] for h in range(2)], axis=1).astype(BF16)
        xt_ref[i] = x
        both = nt(factors, x).astype(BF16)
        left.append(both[:C])
        right.append(both[C:])
    left = jnp.concatenate(left, axis=0)
    for b in range(G):
        row_ref[b, 256:512, :] = left
    right_ref[...] = nn(channel_major(), jnp.concatenate(right, axis=0)).astype(BF16)
    copies[2].wait()
    for b in range(G):
        for i in range(RES):
            for h in range(2):
                at = i * 128 + h * 64 + b * 8
                pair = jnp.concatenate([cot_ref[at : at + 8, :], cot_ref[at + 32 : at + 40, :]], axis=0)
                row_ref[b, i * 32 + h * 16 : i * 32 + h * 16 + 16, :] = pair.astype(BF16)


def swap_to_channels(o):
    n = o.shape[0] // C
    blocks = []
    for e in range(C):
        at = e * 32
        blocks.append(
            jnp.concatenate([o[i * 32 : i * 32 + 32, at : at + 32] for i in range(n)], axis=1)
        )
    return jnp.concatenate(blocks, axis=0)


def swap_to_residues(g):
    n = g.shape[1] // 32
    rows = []
    for i in range(n):
        rows.append(
            jnp.concatenate(
                [g[e * 32 : e * 32 + 32, i * 32 : i * 32 + 32] for e in range(C)], axis=1
            )
        )
    return jnp.concatenate(rows, axis=0)


def right_kernel(row_ref, right_ref, w_ref, col_ref, grads_ref, weight_ref, wide):
    wide[...] = w_ref[...].astype(F32)
    weight = jnp.concatenate([wide[pl.ds(e, 32, stride=32), :] for e in range(C)], axis=0)
    weight_ref[...] = weight.T.astype(BF16)
    weight = weight.astype(BF16)
    for b in range(G):
        grads_ref[b * 256 : b * 256 + 256, :] = swap_to_residues(
            nt(weight, row_ref[b, 0:256, :]).astype(BF16)
        )
    lefts = jnp.concatenate([row_ref[b, 256:512, :] for b in range(G)], axis=0)
    rg = (tn(lefts, grads_ref[...]) * (1.0 / S)).T.reshape(C, G, RES, S)
    for a in range(G):
        col_ref[a, 0:256, :] = rg[:, a].reshape(C * RES, S).astype(BF16)
        col_ref[a, 256:512, :] = right_ref[...]


def left_kernel(row_ref, col_ref, grads_ref, weight_ref, out_ref, gout_ref, outers):
    right = jnp.concatenate(
        [col_ref[a, 256:512, :].astype(F32).reshape(C, RES, S) for a in range(G)], axis=1
    ).reshape(C * G * RES, S).astype(BF16)
    for b in range(G):
        outer = swap_to_channels((nt(row_ref[b, 256:512, :], right) * (1.0 / S)).astype(BF16))
        outers[:, b * 256 : b * 256 + 256] = outer
        out_ref[b, 0:256, :] = nn(weight_ref[...], outer).T.astype(BF16)
        out_ref[b, 256:512, :] = (nn(grads_ref[b * 256 : b * 256 + 256, :], right) * (1.0 / S)).astype(BF16)
    cot = jnp.concatenate([row_ref[b, 0:256, :] for b in range(G)], axis=0)
    gout_ref[...] = nn(outers[...], cot).astype(BF16)


def right_factor_kernel(col_ref, x_ref, right_ref, gr_ref):
    right = sum(col_ref[a, 0:256, :].astype(F32) for a in range(G)).astype(BF16)
    right = tn(channel_major(), right).astype(BF16)
    right_ref[...] = right
    gr_ref[...] = sum(nn(right[i * C : i * C + C], x_ref[i]) for i in range(RES))


def left_factor_kernel(back_ref, gr_ref, x_ref, gout_ref, left_ref, tail_ref):
    left = sum(back_ref[b, 256:512, :].astype(F32) for b in range(G)).astype(BF16)
    left_ref[...] = left
    gl = sum(nn(left[i * C : i * C + C], x_ref[i]) for i in range(RES))
    total = jnp.concatenate([gl, gr_ref[...]], axis=0)
    rows = jnp.concatenate([total[:, 0:128], total[:, 128:256]], axis=0)
    pad = jnp.zeros((4, 128), F32)
    for k in range(C):
        tail_ref[k] = jnp.concatenate(
            [gout_ref[k * 32 : k * 32 + 32, :].astype(F32), rows[k * 4 : k * 4 + 4], pad], axis=0
        ).astype(BF16)


def update_kernel(back_ref, out_ref):
    for b in range(G):
        part = back_ref[b, 0:256, :].astype(F32)
        for i in range(RES):
            for a in range(G):
                at = i * 128 + a * 32 + b * 8
                out_ref[at : at + 8, :] = part[i * 32 + a * 8 : i * 32 + a * 8 + 8, :]


def msa_kernel(left_ref, right_ref, f_ref, out_ref):
    factors = f_ref[...]
    for i in range(RES):
        both = jnp.concatenate([left_ref[i * C : i * C + C, :], right_ref[i * C : i * C + C, :]], axis=0)
        out_ref[i] = tn(both, factors).astype(BF16)


def sum_kernel(in_ref, out_ref):
    total = in_ref[0].astype(F32)
    for k in range(1, in_ref.shape[0]):
        total = total + in_ref[k].astype(F32)
    total = total.astype(BF16)
    for k in range(out_ref.shape[0]):
        out_ref[k] = total


def final_kernel(in_ref, gl_ref, gr_ref, gout_ref, wide):
    scale = 1.0 / 32
    rows = []
    for e in range(C):
        part = in_ref[e].astype(F32) * scale
        wide[e * 32 : e * 32 + 32, :] = part[0:32]
        rows.append(part[32:36])
    for h in range(2):
        for q, out in enumerate((gl_ref, gr_ref)):
            at = h * 16 + q * 8
            out[:, h * 128 : h * 128 + 128] = jnp.concatenate(rows[at : at + 8], axis=0)
    for c in range(C):
        gout_ref[c * 32 : c * 32 + 32, :] = wide[pl.ds(c, 32, stride=32), :]


def per_device(x, f1, f2, w, cot):
    x = x[0].reshape(S * RES, F)
    factors = jnp.concatenate([f1.T, f2.T], axis=0)
    cot = cot[0].reshape(RES * 128, Z)
    row, right, x = call(
        project_kernel,
        [shape((G, 512, S), BF16), shape((256, S), BF16), shape((RES, S, F), BF16)],
        x,
        factors,
        cot,
        scratch=[
            pltpu.VMEM((S * RES, F), BF16),
            pltpu.VMEM((2 * C, F), BF16),
            pltpu.VMEM((RES * 128, Z), F32),
            pltpu.VMEM((2, S * RES, 128), F32),
            pltpu.SemaphoreType.DMA((3,)),
        ],
        flops=33554432,
        hbm=True,
        limit=210,
    )
    row = exchange(row, ROW)
    col, grads, weight = call(
        right_kernel,
        [shape((G, 512, S), BF16), shape((1024, 1024), BF16), shape((128, 1024), BF16)],
        row,
        right,
        w,
        scratch=[pltpu.VMEM((1024, 128), F32)],
        flops=2 * 2 * 1024 * 1024 * 128,
    )
    col = exchange(col, COL)
    back, gout = call(
        left_kernel,
        [shape((G, 512, 128), BF16), shape((1024, 128), BF16)],
        row,
        col,
        grads,
        weight,
        scratch=[pltpu.VMEM((1024, 1024), BF16)],
        flops=4 * 2 * 1024 * 1024 * 128,
    )
    back = exchange(back, ROW)
    right, gr = call(
        right_factor_kernel, [shape((256, S), BF16), shape((C, F), F32)], col, x, flops=33554432
    )
    left, tail = call(
        left_factor_kernel,
        [shape((256, S), BF16), shape((32, 40, 128), BF16)],
        back,
        gr,
        x,
        gout,
        flops=16777216,
    )
    (update,) = call(update_kernel, [shape((RES * 128, Z), F32)], back)
    (msa,) = call(msa_kernel, [shape((RES, S, F), BF16)], left, right, factors, flops=33554432)
    tail = exchange(tail, NEAR)
    (tail,) = call(sum_kernel, [shape((16, 40, 128), BF16)], tail)
    tail = exchange(tail, FAR)
    (tail,) = call(sum_kernel, [shape((32, 40, 128), BF16)], tail)
    tail = exchange(tail, NEAR)
    gl, gr, gout = call(
        final_kernel,
        [shape((C, F), F32), shape((C, F), F32), shape((1024, 128), F32)],
        tail,
        scratch=[pltpu.VMEM((1024, 128), F32)],
    )
    return update.reshape(1, RES, 128, Z), msa.transpose(1, 0, 2)[None], gl.T, gr.T, gout


def solution(mesh):
    split = Mesh(mesh.devices.reshape(4, 4, 2, 4, 2, 2), ("yh", "x", "core", "zh", "zl", "yl"))
    in_specs = (P(DP, None, AXIAL, None), P(), P(), P(), P(DP, AXIAL, None, None))
    out_specs = (P(DP, AXIAL, None, None), P(DP, None, AXIAL, None), P(), P(), P())
    return jax.shard_map(per_device, mesh=split, in_specs=in_specs, out_specs=out_specs, check_vma=False)
```

```python
import jax
import jax.numpy as jnp
from jax import lax
from jax.experimental import pallas as pl
from jax.experimental.pallas import tpu as pltpu
from jax.sharding import Mesh, PartitionSpec as P

BF16 = jnp.bfloat16
F32 = jnp.float32
ROW = ("zl", "yl")
COL = "zh"
NEAR = ("x", "core", "zl", "yl")
FAR = ("zh", "yh")
AXIAL = ("zh", "zl", "yl")
DP = ("yh", "x", "core")

S = 128
RES = 8
C = 32
Z = 128
F = 256
G = 4


def dot(a, b, dims):
    return lax.dot_general(a, b, (dims, ((), ())), preferred_element_type=F32)


def nn(a, b):
    return dot(a, b, ((1,), (0,)))


def nt(a, b):
    return dot(a, b, ((1,), (1,)))


def tn(a, b):
    return dot(a, b, ((0,), (0,)))


def call(kernel, out, *args, scratch=(), flops=0, hbm=False, limit=96):
    size = sum(a.size * a.dtype.itemsize for a in args) + sum(
        o.size * o.dtype.itemsize for o in out
    )
    return pl.pallas_call(
        kernel,
        out_shape=out,
        in_specs=[pl.BlockSpec(memory_space=pltpu.HBM if hbm else pltpu.VMEM)] * len(args),
        out_specs=[pl.BlockSpec(memory_space=pltpu.VMEM)] * len(out),
        scratch_shapes=list(scratch),
        compiler_params=pltpu.CompilerParams(vmem_limit_bytes=limit * 1024 * 256),
        cost_estimate=pl.CostEstimate(flops=flops, bytes_accessed=size, transcendentals=0),
    )(*args)


def shape(dims, dtype):
    return jax.ShapeDtypeStruct(dims, dtype)


def exchange(x, axes):
    return lax.all_to_all(x, axes, split_axis=0, concat_axis=0, tiled=True)


def channel_major():
    n = RES * C
    p = lax.broadcasted_iota(jnp.int32, (n, n), 0)
    q = lax.broadcasted_iota(jnp.int32, (n, n), 1)
    same = ((p >> 3) == (q & 31)) & ((p & 7) == (q >> 5))
    return jnp.where(same, 1.0, 0.0).astype(BF16)


def project_kernel(x_hbm, f_hbm, cot_hbm, row_ref, right_ref, xt_ref, x_ref, f_ref, cot_ref, wide, sems):
    copies = [
        pltpu.make_async_copy(f_hbm, f_ref, sems.at[0]),
        pltpu.make_async_copy(x_hbm, x_ref, sems.at[1]),
        pltpu.make_async_copy(cot_hbm, cot_ref, sems.at[2]),
    ]
    for copy in copies:
        copy.start()
    for copy in copies[:2]:
        copy.wait()
    factors = f_ref[...]
    for h in range(2):
        wide[h] = x_ref[:, h * 128 : h * 128 + 128].astype(F32)
    left, right = [], []
    for i in range(RES):
        x = jnp.concatenate([wide[h, pl.ds(i, S, stride=RES), :] for h in range(2)], axis=1).astype(BF16)
        xt_ref[i] = x
        both = nt(factors, x).astype(BF16)
        left.append(both[:C])
        right.append(both[C:])
    left = jnp.concatenate(left, axis=0)
    for b in range(G):
        row_ref[b, 256:512, :] = left
    right_ref[...] = nn(channel_major(), jnp.concatenate(right, axis=0)).astype(BF16)
    copies[2].wait()
    for b in range(G):
        for i in range(RES):
            for h in range(2):
                at = i * 128 + h * 64 + b * 8
                pair = jnp.concatenate([cot_ref[at : at + 8, :], cot_ref[at + 32 : at + 40, :]], axis=0)
                row_ref[b, i * 32 + h * 16 : i * 32 + h * 16 + 16, :] = pair.astype(BF16)


def swap_blocks(blocks):
    lane = lax.broadcasted_iota(jnp.int32, (32, 128), 1)
    low, even = (lane & 64) == 0, (lane & 32) == 0
    a, b, c, d = blocks
    a, c = jnp.where(low, a, pltpu.roll(c, 64, 1)), jnp.where(low, pltpu.roll(a, 64, 1), c)
    b, d = jnp.where(low, b, pltpu.roll(d, 64, 1)), jnp.where(low, pltpu.roll(b, 64, 1), d)
    a, b = jnp.where(even, a, pltpu.roll(b, 32, 1)), jnp.where(even, pltpu.roll(a, 96, 1), b)
    c, d = jnp.where(even, c, pltpu.roll(d, 32, 1)), jnp.where(even, pltpu.roll(c, 96, 1), d)
    return a, b, c, d


def right_kernel(row_ref, right_ref, w_ref, col_ref, grads_ref, weight_ref, wide):
    wide[...] = w_ref[...].astype(F32)
    weight = jnp.concatenate([wide[pl.ds(e, 32, stride=32), :] for e in range(C)], axis=0)
    weight_ref[...] = weight.T.astype(BF16)
    weight = weight.astype(BF16)
    for b in range(G):
        for at in range(0, 1024, 128):
            grad = nt(weight[at : at + 128], row_ref[b, 0:256, :]).astype(BF16)
            for i in range(RES):
                grads_ref[b * 256 + i * 32 : b * 256 + i * 32 + 32, at : at + 128] = jnp.concatenate(
                    [grad[e * 32 : e * 32 + 32, i * 32 : i * 32 + 32] for e in range(4)], axis=1
                )
    lefts = jnp.concatenate([row_ref[b, 256:512, :] for b in range(G)], axis=0)
    rg = (tn(lefts, grads_ref[...]) * (1.0 / S)).T.reshape(C, G, RES, S)
    for a in range(G):
        col_ref[a, 0:256, :] = rg[:, a].reshape(C * RES, S).astype(BF16)
        col_ref[a, 256:512, :] = right_ref[...]


def left_kernel(row_ref, col_ref, grads_ref, weight_ref, out_ref, gout_ref, outers):
    right = jnp.concatenate(
        [col_ref[a, 256:512, :].astype(F32).reshape(C, RES, S) for a in range(G)], axis=1
    ).reshape(C * G * RES, S).astype(BF16)
    for b in range(G):
        outer = (nt(row_ref[b, 256:512, :], right) * (1.0 / S)).astype(BF16)
        for i in range(0, 256, 128):
            for e in range(0, 1024, 128):
                blocks = [outer[i + q : i + q + 32, e : e + 128] for q in range(0, 128, 32)]
                for q, block in enumerate(swap_blocks(blocks)):
                    outers[e + q * 32 : e + q * 32 + 32, b * 256 + i : b * 256 + i + 128] = block
    for b in range(G):
        out_ref[b, 256:512, :] = (nn(grads_ref[b * 256 : b * 256 + 256, :], right) * (1.0 / S)).astype(BF16)
    update = nn(weight_ref[...], outers[...])
    for b in range(G):
        out_ref[b, 0:256, :] = update[:, b * 256 : b * 256 + 256].T.astype(BF16)
    cot = jnp.concatenate([row_ref[b, 0:256, :] for b in range(G)], axis=0)
    gout_ref[...] = nn(outers[...], cot).astype(BF16)


def factor_kernel(back_ref, col_ref, x_ref, gout_ref, left_ref, right_ref, tail_ref):
    left = sum(back_ref[b, 256:512, :].astype(F32) for b in range(G)).astype(BF16)
    left_ref[...] = left
    right = sum(col_ref[a, 0:256, :].astype(F32) for a in range(G)).astype(BF16)
    right = tn(channel_major(), right).astype(BF16)
    right_ref[...] = right
    total = jnp.zeros((2 * C, F), F32)
    for i in range(RES):
        both = jnp.concatenate([left[i * C : i * C + C], right[i * C : i * C + C]], axis=0)
        total = total + nn(both, x_ref[i])
    rows = jnp.concatenate([total[:, 0:128], total[:, 128:256]], axis=0)
    pad = jnp.zeros((4, 128), F32)
    for k in range(C):
        tail_ref[k] = jnp.concatenate(
            [gout_ref[k * 32 : k * 32 + 32, :].astype(F32), rows[k * 4 : k * 4 + 4], pad], axis=0
        ).astype(BF16)


def update_kernel(back_ref, out_ref):
    for b in range(G):
        part = back_ref[b, 0:256, :].astype(F32)
        for i in range(RES):
            for a in range(G):
                at = i * 128 + a * 32 + b * 8
                out_ref[at : at + 8, :] = part[i * 32 + a * 8 : i * 32 + a * 8 + 8, :]


def msa_kernel(left_ref, right_ref, f_ref, out_ref):
    factors = f_ref[...]
    for i in range(RES):
        both = jnp.concatenate([left_ref[i * C : i * C + C, :], right_ref[i * C : i * C + C, :]], axis=0)
        out_ref[i] = tn(both, factors).astype(BF16)


def sum_kernel(in_ref, out_ref):
    total = in_ref[0].astype(F32)
    for k in range(1, in_ref.shape[0]):
        total = total + in_ref[k].astype(F32)
    total = total.astype(BF16)
    for k in range(out_ref.shape[0]):
        out_ref[k] = total


def final_kernel(in_ref, gl_ref, gr_ref, gout_ref, wide):
    scale = 1.0 / 32
    rows = []
    for e in range(C):
        part = in_ref[e].astype(F32) * scale
        wide[e * 32 : e * 32 + 32, :] = part[0:32]
        rows.append(part[32:36])
    for h in range(2):
        for q, out in enumerate((gl_ref, gr_ref)):
            at = h * 16 + q * 8
            out[:, h * 128 : h * 128 + 128] = jnp.concatenate(rows[at : at + 8], axis=0)
    for c in range(C):
        gout_ref[c * 32 : c * 32 + 32, :] = wide[pl.ds(c, 32, stride=32), :]


def per_device(x, f1, f2, w, cot):
    x = x[0].reshape(S * RES, F)
    factors = jnp.concatenate([f1.T, f2.T], axis=0)
    cot = cot[0].reshape(RES * 128, Z)
    row, right, x = call(
        project_kernel,
        [shape((G, 512, S), BF16), shape((256, S), BF16), shape((RES, S, F), BF16)],
        x,
        factors,
        cot,
        scratch=[
            pltpu.VMEM((S * RES, F), BF16),
            pltpu.VMEM((2 * C, F), BF16),
            pltpu.VMEM((RES * 128, Z), F32),
            pltpu.VMEM((2, S * RES, 128), F32),
            pltpu.SemaphoreType.DMA((3,)),
        ],
        flops=33554432,
        hbm=True,
        limit=210,
    )
    row = exchange(row, ROW)
    col, grads, weight = call(
        right_kernel,
        [shape((G, 512, S), BF16), shape((1024, 1024), BF16), shape((128, 1024), BF16)],
        row,
        right,
        w,
        scratch=[pltpu.VMEM((1024, 128), F32)],
        flops=2 * 2 * 1024 * 1024 * 128,
    )
    col = exchange(col, COL)
    back, gout = call(
        left_kernel,
        [shape((G, 512, 128), BF16), shape((1024, 128), BF16)],
        row,
        col,
        grads,
        weight,
        scratch=[pltpu.VMEM((1024, 1024), BF16)],
        flops=4 * 2 * 1024 * 1024 * 128,
    )
    back = exchange(back, ROW)
    left, right, tail = call(
        factor_kernel,
        [shape((256, S), BF16), shape((256, S), BF16), shape((32, 40, 128), BF16)],
        back,
        col,
        x,
        gout,
        flops=33554432,
    )
    (update,) = call(update_kernel, [shape((RES * 128, Z), F32)], back)
    (msa,) = call(msa_kernel, [shape((RES, S, F), BF16)], left, right, factors, flops=33554432)
    tail = exchange(tail, NEAR)
    (tail,) = call(sum_kernel, [shape((16, 40, 128), BF16)], tail)
    tail = exchange(tail, FAR)
    (tail,) = call(sum_kernel, [shape((32, 40, 128), BF16)], tail)
    tail = exchange(tail, NEAR)
    gl, gr, gout = call(
        final_kernel,
        [shape((C, F), F32), shape((C, F), F32), shape((1024, 128), F32)],
        tail,
        scratch=[pltpu.VMEM((1024, 128), F32)],
    )
    return update.reshape(1, RES, 128, Z), msa.transpose(1, 0, 2)[None], gl.T, gr.T, gout


def solution(mesh):
    split = Mesh(mesh.devices.reshape(4, 4, 2, 4, 2, 2), ("yh", "x", "core", "zh", "zl", "yl"))
    in_specs = (P(DP, None, AXIAL, None), P(), P(), P(), P(DP, AXIAL, None, None))
    out_specs = (P(DP, AXIAL, None, None), P(DP, None, AXIAL, None), P(), P(), P())
    return jax.shard_map(per_device, mesh=split, in_specs=in_specs, out_specs=out_specs, check_vma=False)
```

```python
import jax
import jax.numpy as jnp
from jax import lax
from jax.experimental import pallas as pl
from jax.experimental.pallas import tpu as pltpu
from jax.sharding import Mesh, PartitionSpec as P

BF16 = jnp.bfloat16
F32 = jnp.float32
ROW = ("zl", "yl")
COL = "zh"
NEAR = ("x", "core", "zl", "yl")
NEAREST = ("x", "zl", "yl")
FAR = ("zh", "yh")
AXIAL = ("zh", "zl", "yl")
DP = ("yh", "x", "core")

S = 128
RES = 8
C = 32
Z = 128
F = 256
G = 4


def dot(a, b, dims):
    return lax.dot_general(a, b, (dims, ((), ())), preferred_element_type=F32)


def nn(a, b):
    return dot(a, b, ((1,), (0,)))


def nt(a, b):
    return dot(a, b, ((1,), (1,)))


def tn(a, b):
    return dot(a, b, ((0,), (0,)))


def call(kernel, out, *args, scratch=(), flops=0, hbm=False, limit=96, aliases=None):
    size = sum(a.size * a.dtype.itemsize for a in args) + sum(
        o.size * o.dtype.itemsize for o in out
    )
    return pl.pallas_call(
        kernel,
        out_shape=out,
        in_specs=[pl.BlockSpec(memory_space=pltpu.HBM if hbm else pltpu.VMEM)] * len(args),
        out_specs=[pl.BlockSpec(memory_space=pltpu.VMEM)] * len(out),
        scratch_shapes=list(scratch),
        input_output_aliases=aliases or {},
        compiler_params=pltpu.CompilerParams(vmem_limit_bytes=limit * 1024 * 256),
        cost_estimate=pl.CostEstimate(flops=flops, bytes_accessed=size, transcendentals=0),
    )(*args)


def shape(dims, dtype):
    return jax.ShapeDtypeStruct(dims, dtype)


def exchange(x, axes):
    return lax.all_to_all(x, axes, split_axis=0, concat_axis=0, tiled=True)


def channel_major():
    n = RES * C
    p = lax.broadcasted_iota(jnp.int32, (n, n), 0)
    q = lax.broadcasted_iota(jnp.int32, (n, n), 1)
    same = ((p >> 3) == (q & 31)) & ((p & 7) == (q >> 5))
    return jnp.where(same, 1.0, 0.0).astype(BF16)


def pack_kernel(x_hbm, cot_hbm, row_ref, xt_ref, x_ref, cot_ref, wide, sems):
    copies = [
        pltpu.make_async_copy(x_hbm, x_ref, sems.at[0]),
        pltpu.make_async_copy(cot_hbm, cot_ref, sems.at[1]),
    ]
    for copy in copies:
        copy.start()
    copies[0].wait()
    for h in range(2):
        wide[h] = x_ref[:, h * 128 : h * 128 + 128].astype(F32)
    for i in range(RES):
        for h in range(2):
            xt_ref[i, :, h * 128 : h * 128 + 128] = wide[h, pl.ds(i, S, stride=RES), :].astype(BF16)
    copies[1].wait()
    for b in range(G):
        for i in range(RES):
            for h in range(2):
                at = i * 128 + h * 64 + b * 8
                pair = jnp.concatenate([cot_ref[at : at + 8, :], cot_ref[at + 32 : at + 40, :]], axis=0)
                row_ref[b, i * 32 + h * 16 : i * 32 + h * 16 + 16, :] = pair.astype(BF16)


def project_kernel(row_in, x_ref, f1_ref, f2_ref, row_ref, right_ref):
    del row_in
    factors = jnp.concatenate([f1_ref[...], f2_ref[...]], axis=0)
    left, right = [], []
    for i in range(RES):
        both = nt(factors, x_ref[i]).astype(BF16)
        left.append(both[:C])
        right.append(both[C:])
    left = jnp.concatenate(left, axis=0)
    for b in range(G):
        row_ref[b, 256:512, :] = left
    right_ref[...] = nn(channel_major(), jnp.concatenate(right, axis=0)).astype(BF16)


def swap_blocks(blocks):
    lane = lax.broadcasted_iota(jnp.int32, (32, 128), 1)
    low, even = (lane & 64) == 0, (lane & 32) == 0
    a, b, c, d = blocks
    a, c = jnp.where(low, a, pltpu.roll(c, 64, 1)), jnp.where(low, pltpu.roll(a, 64, 1), c)
    b, d = jnp.where(low, b, pltpu.roll(d, 64, 1)), jnp.where(low, pltpu.roll(b, 64, 1), d)
    a, b = jnp.where(even, a, pltpu.roll(b, 32, 1)), jnp.where(even, pltpu.roll(a, 96, 1), b)
    c, d = jnp.where(even, c, pltpu.roll(d, 32, 1)), jnp.where(even, pltpu.roll(c, 96, 1), d)
    return a, b, c, d


def right_kernel(row_ref, right_ref, w_ref, col_ref, grads_ref, weight_ref, wide):
    wide[...] = w_ref[...].astype(F32)
    weight = jnp.concatenate([wide[pl.ds(e, 32, stride=32), :] for e in range(C)], axis=0)
    weight_ref[...] = weight.T.astype(BF16)
    weight = weight.astype(BF16)
    for b in range(G):
        for at in range(0, 1024, 128):
            grad = nt(weight[at : at + 128], row_ref[b, 0:256, :]).astype(BF16)
            for i in range(RES):
                grads_ref[b * 256 + i * 32 : b * 256 + i * 32 + 32, at : at + 128] = jnp.concatenate(
                    [grad[e * 32 : e * 32 + 32, i * 32 : i * 32 + 32] for e in range(4)], axis=1
                )
    lefts = jnp.concatenate([row_ref[b, 256:512, :] for b in range(G)], axis=0)
    rg = (tn(lefts, grads_ref[...]) * (1.0 / S)).T.reshape(C, G, RES, S)
    for a in range(G):
        col_ref[a, 0:256, :] = rg[:, a].reshape(C * RES, S).astype(BF16)
        col_ref[a, 256:512, :] = right_ref[...]


def left_kernel(row_ref, col_ref, grads_ref, weight_ref, out_ref, gout_ref, outers):
    right = jnp.concatenate(
        [col_ref[a, 256:512, :].astype(F32).reshape(C, RES, S) for a in range(G)], axis=1
    ).reshape(C * G * RES, S).astype(BF16)
    for b in range(G):
        outer = (nt(row_ref[b, 256:512, :], right) * (1.0 / S)).astype(BF16)
        for i in range(0, 256, 128):
            for e in range(0, 1024, 128):
                blocks = [outer[i + q : i + q + 32, e : e + 128] for q in range(0, 128, 32)]
                for q, block in enumerate(swap_blocks(blocks)):
                    outers[e + q * 32 : e + q * 32 + 32, b * 256 + i : b * 256 + i + 128] = block
    for b in range(G):
        out_ref[b, 256:512, :] = (nn(grads_ref[b * 256 : b * 256 + 256, :], right) * (1.0 / S)).astype(BF16)
    update = nn(weight_ref[...], outers[...])
    for b in range(G):
        out_ref[b, 0:256, :] = update[:, b * 256 : b * 256 + 256].T.astype(BF16)
    cot = jnp.concatenate([row_ref[b, 0:256, :] for b in range(G)], axis=0)
    gout_ref[...] = nn(outers[...], cot).astype(BF16)


def factor_kernel(back_ref, col_ref, x_ref, gout_ref, other_ref, left_ref, right_ref, tail_ref):
    left = sum(back_ref[b, 256:512, :].astype(F32) for b in range(G)).astype(BF16)
    left_ref[...] = left
    right = sum(col_ref[a, 0:256, :].astype(F32) for a in range(G)).astype(BF16)
    right = tn(channel_major(), right).astype(BF16)
    right_ref[...] = right
    total = jnp.zeros((2 * C, F), F32)
    for i in range(RES):
        both = jnp.concatenate([left[i * C : i * C + C], right[i * C : i * C + C]], axis=0)
        total = total + nn(both, x_ref[i])
    rows = jnp.concatenate([total[:, 0:128], total[:, 128:256]], axis=0)
    half = pl.ds(pl.multiple_of(lax.axis_index("core") * 512, 512), 512)
    gout = gout_ref[half, :].astype(F32) + other_ref[half, :].astype(F32)
    for k in range(16):
        tail_ref[k] = jnp.concatenate([gout[k * 32 : k * 32 + 32], rows[k * 8 : k * 8 + 8]], axis=0).astype(BF16)


def update_kernel(back_ref, out_ref):
    for b in range(G):
        part = back_ref[b, 0:256, :].astype(F32)
        for i in range(RES):
            for a in range(G):
                at = i * 128 + a * 32 + b * 8
                out_ref[at : at + 8, :] = part[i * 32 + a * 8 : i * 32 + a * 8 + 8, :]


def msa_kernel(left_ref, right_ref, f1_ref, f2_ref, out_ref):
    factors = jnp.concatenate([f1_ref[...], f2_ref[...]], axis=0)
    for i in range(RES):
        both = jnp.concatenate([left_ref[i * C : i * C + C, :], right_ref[i * C : i * C + C, :]], axis=0)
        out_ref[i] = tn(both, factors).astype(BF16)


def sum_kernel(in_ref, out_ref):
    total = in_ref[0].astype(F32)
    for k in range(1, in_ref.shape[0]):
        total = total + in_ref[k].astype(F32)
    total = total.astype(BF16)
    for k in range(out_ref.shape[0]):
        out_ref[k] = total


def final_kernel(in_ref, gl_ref, gr_ref, gout_ref, wide):
    scale = 1.0 / 32
    rows = []
    for k in range(16):
        at = k // 4 * 8 + k % 4
        parts = [in_ref[at + core * 4].astype(F32) * scale for core in range(2)]
        for core in range(2):
            wide[(core * 16 + k) * 32 : (core * 16 + k) * 32 + 32, :] = parts[core][0:32]
        rows.append(parts[0][32:40] + parts[1][32:40])
    for h in range(2):
        for q, out in enumerate((gl_ref, gr_ref)):
            at = h * 8 + q * 4
            out[:, h * 128 : h * 128 + 128] = jnp.concatenate(rows[at : at + 4], axis=0)
    for c in range(C):
        gout_ref[c * 32 : c * 32 + 32, :] = wide[pl.ds(c, 32, stride=32), :]


def per_device(x, f1, f2, w, cot):
    x = x[0].reshape(S * RES, F)
    f1, f2 = f1.T, f2.T
    cot = cot[0].reshape(RES * 128, Z)
    row, x = call(
        pack_kernel,
        [shape((G, 512, S), BF16), shape((RES, S, F), BF16)],
        x,
        cot,
        scratch=[
            pltpu.VMEM((S * RES, F), BF16),
            pltpu.VMEM((RES * 128, Z), F32),
            pltpu.VMEM((2, S * RES, 128), F32),
            pltpu.SemaphoreType.DMA((2,)),
        ],
        hbm=True,
        limit=210,
        flops=2 * 10**9,
    )
    row, right = call(
        project_kernel,
        [shape((G, 512, S), BF16), shape((256, S), BF16)],
        row,
        x,
        f1,
        f2,
        flops=33554432,
        aliases={0: 0},
    )
    row = exchange(row, ROW)
    col, grads, weight = call(
        right_kernel,
        [shape((G, 512, S), BF16), shape((1024, 1024), BF16), shape((128, 1024), BF16)],
        row,
        right,
        w,
        scratch=[pltpu.VMEM((1024, 128), F32)],
        flops=2 * 2 * 1024 * 1024 * 128,
    )
    col = exchange(col, COL)
    back, gout = call(
        left_kernel,
        [shape((G, 512, 128), BF16), shape((1024, 128), BF16)],
        row,
        col,
        grads,
        weight,
        scratch=[pltpu.VMEM((1024, 1024), BF16)],
        flops=4 * 2 * 1024 * 1024 * 128,
    )
    other = lax.ppermute(gout, "core", [(0, 1), (1, 0)])
    back = exchange(back, ROW)
    left, right, tail = call(
        factor_kernel,
        [shape((256, S), BF16), shape((256, S), BF16), shape((16, 40, 128), BF16)],
        back,
        col,
        x,
        gout,
        other,
        flops=33554432,
    )
    (update,) = call(update_kernel, [shape((RES * 128, Z), F32)], back)
    (msa,) = call(msa_kernel, [shape((RES, S, F), BF16)], left, right, f1, f2, flops=33554432)
    tail = exchange(tail, NEAREST)
    (tail,) = call(sum_kernel, [shape((16, 40, 128), BF16)], tail)
    tail = exchange(tail, FAR)
    (tail,) = call(sum_kernel, [shape((32, 40, 128), BF16)], tail)
    tail = exchange(tail, NEAR)
    gl, gr, gout = call(
        final_kernel,
        [shape((C, F), F32), shape((C, F), F32), shape((1024, 128), F32)],
        tail,
        scratch=[pltpu.VMEM((1024, 128), F32)],
    )
    return update.reshape(1, RES, 128, Z), msa.transpose(1, 0, 2)[None], gl.T, gr.T, gout


def solution(mesh):
    split = Mesh(mesh.devices.reshape(4, 4, 2, 4, 2, 2), ("yh", "x", "core", "zh", "zl", "yl"))
    in_specs = (P(DP, None, AXIAL, None), P(), P(), P(), P(DP, AXIAL, None, None))
    out_specs = (P(DP, AXIAL, None, None), P(DP, None, AXIAL, None), P(), P(), P())
    return jax.shard_map(per_device, mesh=split, in_specs=in_specs, out_specs=out_specs, check_vma=False)
```

```python
import jax
import jax.numpy as jnp
from jax import lax
from jax.experimental import pallas as pl
from jax.experimental.pallas import tpu as pltpu
from jax.sharding import Mesh, PartitionSpec as P

BF16 = jnp.bfloat16
F32 = jnp.float32
ROW = ("zl", "yl")
COL = "zh"
NEAR = ("x", "core", "zl", "yl")
NEAREST = ("x", "zl", "yl")
FAR = ("zh", "yh")
AXIAL = ("zh", "zl", "yl")
DP = ("yh", "x", "core")

S = 128
RES = 8
C = 32
Z = 128
F = 256
G = 4


def dot(a, b, dims):
    return lax.dot_general(a, b, (dims, ((), ())), preferred_element_type=F32)


def nn(a, b):
    return dot(a, b, ((1,), (0,)))


def nt(a, b):
    return dot(a, b, ((1,), (1,)))


def tn(a, b):
    return dot(a, b, ((0,), (0,)))


def call(kernel, out, *args, scratch=(), flops=0, hbm=False, limit=96, aliases=None):
    size = sum(a.size * a.dtype.itemsize for a in args) + sum(
        o.size * o.dtype.itemsize for o in out
    )
    return pl.pallas_call(
        kernel,
        out_shape=out,
        in_specs=[pl.BlockSpec(memory_space=pltpu.HBM if hbm else pltpu.VMEM)] * len(args),
        out_specs=[pl.BlockSpec(memory_space=pltpu.VMEM)] * len(out),
        scratch_shapes=list(scratch),
        input_output_aliases=aliases or {},
        compiler_params=pltpu.CompilerParams(vmem_limit_bytes=limit * 1024 * 256),
        cost_estimate=pl.CostEstimate(flops=flops, bytes_accessed=size, transcendentals=0),
    )(*args)


def shape(dims, dtype):
    return jax.ShapeDtypeStruct(dims, dtype)


def exchange(x, axes):
    return lax.all_to_all(x, axes, split_axis=0, concat_axis=0, tiled=True)


def channel_major():
    n = RES * C
    p = lax.broadcasted_iota(jnp.int32, (n, n), 0)
    q = lax.broadcasted_iota(jnp.int32, (n, n), 1)
    same = ((p >> 3) == (q & 31)) & ((p & 7) == (q >> 5))
    return jnp.where(same, 1.0, 0.0).astype(BF16)


def pack_kernel(x_hbm, cot_hbm, row_ref, xt_ref, x_ref, cot_ref, wide, sems):
    loads = []
    for k in range(2):
        part = pl.ds(k * 512, 512)
        loads.append(pltpu.make_async_copy(x_hbm.at[part], x_ref.at[part], sems.at[k]))
    for k in range(2):
        part = pl.ds(k * 512, 512)
        loads.append(pltpu.make_async_copy(cot_hbm.at[part], cot_ref.at[part], sems.at[2 + k]))
    for load in loads:
        load.start()
    for k in range(2):
        loads[k].wait()
        for h in range(2):
            wide[h, k * 512 : k * 512 + 512, :] = x_ref[k * 512 : k * 512 + 512, h * 128 : h * 128 + 128].astype(F32)
        for i in range(RES):
            for h in range(2):
                xt_ref[i, k * 64 : k * 64 + 64, h * 128 : h * 128 + 128] = wide[
                    h, pl.ds(k * 512 + i, 64, stride=RES), :
                ].astype(BF16)
    for k in range(2):
        loads[2 + k].wait()
        for b in range(G):
            for i in range(k * 4, k * 4 + 4):
                for h in range(2):
                    at = i * 128 + h * 64 + b * 8
                    pair = jnp.concatenate([cot_ref[at : at + 8, :], cot_ref[at + 32 : at + 40, :]], axis=0)
                    row_ref[b, i * 32 + h * 16 : i * 32 + h * 16 + 16, :] = pair.astype(BF16)


def project_kernel(row_in, x_ref, f1_ref, f2_ref, row_ref, right_ref):
    del row_in
    factors = jnp.concatenate([f1_ref[...], f2_ref[...]], axis=0)
    left, right = [], []
    for i in range(RES):
        both = nt(factors, x_ref[i]).astype(BF16)
        left.append(both[:C])
        right.append(both[C:])
    left = jnp.concatenate(left, axis=0)
    for b in range(G):
        row_ref[b, 256:512, :] = left
    right_ref[...] = nn(channel_major(), jnp.concatenate(right, axis=0)).astype(BF16)


def swap_blocks(blocks):
    lane = lax.broadcasted_iota(jnp.int32, (32, 128), 1)
    low, even = (lane & 64) == 0, (lane & 32) == 0
    a, b, c, d = blocks
    a, c = jnp.where(low, a, pltpu.roll(c, 64, 1)), jnp.where(low, pltpu.roll(a, 64, 1), c)
    b, d = jnp.where(low, b, pltpu.roll(d, 64, 1)), jnp.where(low, pltpu.roll(b, 64, 1), d)
    a, b = jnp.where(even, a, pltpu.roll(b, 32, 1)), jnp.where(even, pltpu.roll(a, 96, 1), b)
    c, d = jnp.where(even, c, pltpu.roll(d, 32, 1)), jnp.where(even, pltpu.roll(c, 96, 1), d)
    return a, b, c, d


def right_kernel(row_ref, right_ref, w_ref, col_ref, grads_ref, weight_ref, wide):
    wide[...] = w_ref[...].astype(F32)
    weight = jnp.concatenate([wide[pl.ds(e, 32, stride=32), :] for e in range(C)], axis=0)
    weight_ref[...] = weight.T.astype(BF16)
    weight = weight.astype(BF16)
    for b in range(G):
        for at in range(0, 1024, 128):
            grad = nt(weight[at : at + 128], row_ref[b, 0:256, :]).astype(BF16)
            for i in range(RES):
                grads_ref[b * 256 + i * 32 : b * 256 + i * 32 + 32, at : at + 128] = jnp.concatenate(
                    [grad[e * 32 : e * 32 + 32, i * 32 : i * 32 + 32] for e in range(4)], axis=1
                )
    lefts = jnp.concatenate([row_ref[b, 256:512, :] for b in range(G)], axis=0)
    rg = (tn(lefts, grads_ref[...]) * (1.0 / S)).T.reshape(C, G, RES, S)
    for a in range(G):
        col_ref[a, 0:256, :] = rg[:, a].reshape(C * RES, S).astype(BF16)
        col_ref[a, 256:512, :] = right_ref[...]


def left_kernel(row_ref, col_ref, grads_ref, weight_ref, out_ref, update_ref, gout_ref, outers):
    right = jnp.concatenate(
        [col_ref[a, 256:512, :].astype(F32).reshape(C, RES, S) for a in range(G)], axis=1
    ).reshape(C * G * RES, S).astype(BF16)
    for b in range(G):
        outer = (nt(row_ref[b, 256:512, :], right) * (1.0 / S)).astype(BF16)
        for i in range(0, 256, 128):
            for e in range(0, 1024, 128):
                blocks = [outer[i + q : i + q + 32, e : e + 128] for q in range(0, 128, 32)]
                for q, block in enumerate(swap_blocks(blocks)):
                    outers[e + q * 32 : e + q * 32 + 32, b * 256 + i : b * 256 + i + 128] = block
    for b in range(G):
        out_ref[b] = (nn(grads_ref[b * 256 : b * 256 + 256, :], right) * (1.0 / S)).astype(BF16)
    update = nn(weight_ref[...], outers[...])
    for b in range(G):
        update_ref[b] = update[:, b * 256 : b * 256 + 256].T.astype(BF16)
    cot = jnp.concatenate([row_ref[b, 0:256, :] for b in range(G)], axis=0)
    gout_ref[...] = nn(outers[...], cot).astype(BF16)


def factor_kernel(back_ref, col_ref, x_ref, gout_ref, other_ref, left_ref, right_ref, tail_ref):
    left = sum(back_ref[b].astype(F32) for b in range(G)).astype(BF16)
    left_ref[...] = left
    right = sum(col_ref[a, 0:256, :].astype(F32) for a in range(G)).astype(BF16)
    right = tn(channel_major(), right).astype(BF16)
    right_ref[...] = right
    total = jnp.zeros((2 * C, F), F32)
    for i in range(RES):
        both = jnp.concatenate([left[i * C : i * C + C], right[i * C : i * C + C]], axis=0)
        total = total + nn(both, x_ref[i])
    rows = jnp.concatenate([total[:, 0:128], total[:, 128:256]], axis=0)
    half = pl.ds(pl.multiple_of(lax.axis_index("core") * 512, 512), 512)
    gout = gout_ref[half, :].astype(F32) + other_ref[half, :].astype(F32)
    for k in range(16):
        tail_ref[k] = jnp.concatenate([gout[k * 32 : k * 32 + 32], rows[k * 8 : k * 8 + 8]], axis=0).astype(BF16)


def place():
    return lax.axis_index("zl") * 2 + lax.axis_index("yl")


def split_kernel(in_ref, update_ref, out_ref, *part_refs):
    sum_kernel(in_ref, out_ref)
    me = place()
    for k, ref in enumerate(part_refs):
        ref[...] = update_ref[lax.bitwise_xor(me, k)]


def join_kernel(in_ref, *refs):
    sum_kernel(in_ref, refs[G])
    me = place()
    for k in range(G):
        refs[G + 1][lax.bitwise_xor(me, k)] = refs[k][...]


def update_kernel(update_ref, out_ref):
    for b in range(G):
        part = update_ref[b].astype(F32)
        for i in range(RES):
            for a in range(G):
                at = i * 128 + a * 32 + b * 8
                out_ref[at : at + 8, :] = part[i * 32 + a * 8 : i * 32 + a * 8 + 8, :]


def msa_kernel(left_ref, right_ref, f1_ref, f2_ref, out_ref):
    factors = jnp.concatenate([f1_ref[...], f2_ref[...]], axis=0)
    for i in range(RES):
        both = jnp.concatenate([left_ref[i * C : i * C + C, :], right_ref[i * C : i * C + C, :]], axis=0)
        out_ref[i] = tn(both, factors).astype(BF16)


def sum_kernel(in_ref, out_ref):
    total = in_ref[0].astype(F32)
    for k in range(1, in_ref.shape[0]):
        total = total + in_ref[k].astype(F32)
    total = total.astype(BF16)
    for k in range(out_ref.shape[0]):
        out_ref[k] = total


def final_kernel(in_ref, gl_ref, gr_ref, gout_ref, wide):
    scale = 1.0 / 32
    rows = []
    for k in range(16):
        at = k // 4 * 8 + k % 4
        parts = [in_ref[at + core * 4].astype(F32) * scale for core in range(2)]
        for core in range(2):
            wide[(core * 16 + k) * 32 : (core * 16 + k) * 32 + 32, :] = parts[core][0:32]
        rows.append(parts[0][32:40] + parts[1][32:40])
    for h in range(2):
        for q, out in enumerate((gl_ref, gr_ref)):
            at = h * 8 + q * 4
            out[:, h * 128 : h * 128 + 128] = jnp.concatenate(rows[at : at + 4], axis=0)
    for c in range(C):
        gout_ref[c * 32 : c * 32 + 32, :] = wide[pl.ds(c, 32, stride=32), :]


def per_device(x, f1, f2, w, cot):
    x = x[0].reshape(S * RES, F)
    f1, f2 = f1.T, f2.T
    cot = cot[0].reshape(RES * 128, Z)
    row, x = call(
        pack_kernel,
        [shape((G, 512, S), BF16), shape((RES, S, F), BF16)],
        x,
        cot,
        scratch=[
            pltpu.VMEM((S * RES, F), BF16),
            pltpu.VMEM((RES * 128, Z), F32),
            pltpu.VMEM((2, S * RES, 128), F32),
            pltpu.SemaphoreType.DMA((4,)),
        ],
        hbm=True,
        limit=210,
        flops=2 * 10**9,
    )
    row, right = call(
        project_kernel,
        [shape((G, 512, S), BF16), shape((256, S), BF16)],
        row,
        x,
        f1,
        f2,
        flops=33554432,
        aliases={0: 0},
    )
    row = exchange(row, ROW)
    col, grads, weight = call(
        right_kernel,
        [shape((G, 512, S), BF16), shape((1024, 1024), BF16), shape((128, 1024), BF16)],
        row,
        right,
        w,
        scratch=[pltpu.VMEM((1024, 128), F32)],
        flops=2 * 2 * 1024 * 1024 * 128,
    )
    col = exchange(col, COL)
    back, update, gout = call(
        left_kernel,
        [shape((G, 256, 128), BF16), shape((G, 256, 128), BF16), shape((1024, 128), BF16)],
        row,
        col,
        grads,
        weight,
        scratch=[pltpu.VMEM((1024, 1024), BF16)],
        flops=4 * 2 * 1024 * 1024 * 128,
    )
    other = lax.ppermute(gout, "core", [(0, 1), (1, 0)])
    back = exchange(back, ROW)
    left, right, tail = call(
        factor_kernel,
        [shape((256, S), BF16), shape((256, S), BF16), shape((16, 40, 128), BF16)],
        back,
        col,
        x,
        gout,
        other,
        flops=33554432,
    )
    (msa,) = call(msa_kernel, [shape((RES, S, F), BF16)], left, right, f1, f2, flops=33554432)
    tail = exchange(tail, NEAREST)
    tail, *updates = call(
        split_kernel, [shape((16, 40, 128), BF16)] + [shape((256, 128), BF16)] * G, tail, update
    )
    tail = exchange(tail, FAR)
    updates = [lax.ppermute(u, ROW, [(b, b ^ k) for b in range(G)]) if k else u for k, u in enumerate(updates)]
    tail, update = call(
        join_kernel, [shape((32, 40, 128), BF16), shape((G, 256, 128), BF16)], tail, *updates
    )
    (update,) = call(update_kernel, [shape((RES * 128, Z), F32)], update)
    tail = exchange(tail, NEAR)
    gl, gr, gout = call(
        final_kernel,
        [shape((C, F), F32), shape((C, F), F32), shape((1024, 128), F32)],
        tail,
        scratch=[pltpu.VMEM((1024, 128), F32)],
    )
    return update.reshape(1, RES, 128, Z), msa.transpose(1, 0, 2)[None], gl.T, gr.T, gout


def solution(mesh):
    split = Mesh(mesh.devices.reshape(4, 4, 2, 4, 2, 2), ("yh", "x", "core", "zh", "zl", "yl"))
    in_specs = (P(DP, None, AXIAL, None), P(), P(), P(), P(DP, AXIAL, None, None))
    out_specs = (P(DP, AXIAL, None, None), P(DP, None, AXIAL, None), P(), P(), P())
    return jax.shard_map(per_device, mesh=split, in_specs=in_specs, out_specs=out_specs, check_vma=False)
```

```python
import jax
import jax.numpy as jnp
from jax import lax
from jax.experimental import pallas as pl
from jax.experimental.pallas import tpu as pltpu
from jax.sharding import Mesh, PartitionSpec as P

BF16 = jnp.bfloat16
F32 = jnp.float32
ROW = ("zl", "yl")
COL = "zh"
NEAR = ("x", "core", "zl", "yl")
NEAREST = ("x", "zl", "yl")
FAR = ("zh", "yh")
AXIAL = ("zh", "zl", "yl")
DP = ("yh", "x", "core")

S = 128
RES = 8
C = 32
Z = 128
F = 256
G = 4


def dot(a, b, dims):
    return lax.dot_general(a, b, (dims, ((), ())), preferred_element_type=F32)


def nn(a, b):
    return dot(a, b, ((1,), (0,)))


def nt(a, b):
    return dot(a, b, ((1,), (1,)))


def tn(a, b):
    return dot(a, b, ((0,), (0,)))


def call(kernel, out, *args, scratch=(), flops=0, hbm=False, limit=96, aliases=None):
    size = sum(a.size * a.dtype.itemsize for a in args) + sum(
        o.size * o.dtype.itemsize for o in out
    )
    return pl.pallas_call(
        kernel,
        out_shape=out,
        in_specs=[pl.BlockSpec(memory_space=pltpu.HBM if hbm else pltpu.VMEM)] * len(args),
        out_specs=[pl.BlockSpec(memory_space=pltpu.VMEM)] * len(out),
        scratch_shapes=list(scratch),
        input_output_aliases=aliases or {},
        compiler_params=pltpu.CompilerParams(vmem_limit_bytes=limit * 1024 * 256),
        cost_estimate=pl.CostEstimate(flops=flops, bytes_accessed=size, transcendentals=0),
    )(*args)


def shape(dims, dtype):
    return jax.ShapeDtypeStruct(dims, dtype)


def exchange(x, axes):
    return lax.all_to_all(x, axes, split_axis=0, concat_axis=0, tiled=True)


def channel_major():
    n = RES * C
    p = lax.broadcasted_iota(jnp.int32, (n, n), 0)
    q = lax.broadcasted_iota(jnp.int32, (n, n), 1)
    same = ((p >> 3) == (q & 31)) & ((p & 7) == (q >> 5))
    return jnp.where(same, 1.0, 0.0).astype(BF16)


def pack_kernel(x_hbm, cot_hbm, row_ref, xt_ref, x_ref, cot_ref, wide, sems):
    loads = []
    for k in range(2):
        part = pl.ds(k * 512, 512)
        loads.append(pltpu.make_async_copy(x_hbm.at[part], x_ref.at[part], sems.at[k]))
    for k in range(2):
        part = pl.ds(k * 512, 512)
        loads.append(pltpu.make_async_copy(cot_hbm.at[part], cot_ref.at[part], sems.at[2 + k]))
    for load in loads:
        load.start()
    for k in range(2):
        loads[k].wait()
        for h in range(2):
            wide[h, k * 512 : k * 512 + 512, :] = x_ref[k * 512 : k * 512 + 512, h * 128 : h * 128 + 128].astype(F32)
        for i in range(RES):
            for h in range(2):
                xt_ref[i, k * 64 : k * 64 + 64, h * 128 : h * 128 + 128] = wide[
                    h, pl.ds(k * 512 + i, 64, stride=RES), :
                ].astype(BF16)
    for k in range(2):
        loads[2 + k].wait()
        for b in range(G):
            for i in range(k * 4, k * 4 + 4):
                for h in range(2):
                    at = i * 128 + h * 64 + b * 8
                    pair = jnp.concatenate([cot_ref[at : at + 8, :], cot_ref[at + 32 : at + 40, :]], axis=0)
                    row_ref[b, i * 32 + h * 16 : i * 32 + h * 16 + 16, :] = pair.astype(BF16)


def project_kernel(row_in, x_ref, f1_ref, f2_ref, row_ref, right_ref):
    del row_in
    factors = jnp.concatenate([f1_ref[...], f2_ref[...]], axis=0)
    left, right = [], []
    for i in range(RES):
        both = nt(factors, x_ref[i]).astype(BF16)
        left.append(both[:C])
        right.append(both[C:])
    left = jnp.concatenate(left, axis=0)
    for b in range(G):
        row_ref[b, 256:512, :] = left
    right_ref[...] = nn(channel_major(), jnp.concatenate(right, axis=0)).astype(BF16)


def swap_blocks(blocks):
    lane = lax.broadcasted_iota(jnp.int32, (32, 128), 1)
    low, even = (lane & 64) == 0, (lane & 32) == 0
    a, b, c, d = blocks
    a, c = jnp.where(low, a, pltpu.roll(c, 64, 1)), jnp.where(low, pltpu.roll(a, 64, 1), c)
    b, d = jnp.where(low, b, pltpu.roll(d, 64, 1)), jnp.where(low, pltpu.roll(b, 64, 1), d)
    a, b = jnp.where(even, a, pltpu.roll(b, 32, 1)), jnp.where(even, pltpu.roll(a, 96, 1), b)
    c, d = jnp.where(even, c, pltpu.roll(d, 32, 1)), jnp.where(even, pltpu.roll(c, 96, 1), d)
    return a, b, c, d


def right_kernel(row_ref, right_ref, w_ref, col_ref, grads_ref, weight_ref, wide):
    wide[0:1024, :] = w_ref[...].astype(F32)
    weight = jnp.concatenate([wide[pl.ds(e, 32, stride=32), :] for e in range(C)], axis=0)
    weight_ref[...] = weight.T.astype(BF16)
    weight = weight.astype(BF16)
    for b in range(G):
        for at in range(0, 1024, 128):
            grad = nt(weight[at : at + 128], row_ref[b, 0:256, :]).astype(BF16)
            for i in range(RES):
                grads_ref[b * 256 + i * 32 : b * 256 + i * 32 + 32, at : at + 128] = jnp.concatenate(
                    [grad[e * 32 : e * 32 + 32, i * 32 : i * 32 + 32] for e in range(4)], axis=1
                )
    lefts = jnp.concatenate([row_ref[b, 256:512, :] for b in range(G)], axis=0)
    rg = (tn(lefts, grads_ref[...]) * (1.0 / S)).T.reshape(C, G, RES, S)
    for a in range(G):
        col_ref[a, 0:256, :] = rg[:, a].reshape(C * RES, S).astype(BF16)
        col_ref[a, 256:512, :] = right_ref[...]


def left_kernel(row_ref, col_ref, grads_ref, weight_ref, out_ref, update_ref, gout_ref, outers):
    right = jnp.concatenate(
        [col_ref[a, 256:512, :].astype(F32).reshape(C, RES, S) for a in range(G)], axis=1
    ).reshape(C * G * RES, S).astype(BF16)
    for b in range(G):
        outer = (nt(row_ref[b, 256:512, :], right) * (1.0 / S)).astype(BF16)
        for i in range(0, 256, 128):
            for e in range(0, 1024, 128):
                blocks = [outer[i + q : i + q + 32, e : e + 128] for q in range(0, 128, 32)]
                for q, block in enumerate(swap_blocks(blocks)):
                    outers[e + q * 32 : e + q * 32 + 32, b * 256 + i : b * 256 + i + 128] = block
    for b in range(G):
        out_ref[b] = (nn(grads_ref[b * 256 : b * 256 + 256, :], right) * (1.0 / S)).astype(BF16)
    update = nn(weight_ref[...], outers[...])
    for b in range(G):
        update_ref[b] = update[:, b * 256 : b * 256 + 256].T.astype(BF16)
    cot = jnp.concatenate([row_ref[b, 0:256, :] for b in range(G)], axis=0)
    gout_ref[...] = nn(outers[...], cot).astype(BF16)


def factor_kernel(back_ref, col_ref, x_ref, gout_ref, other_ref, left_ref, right_ref, tail_ref):
    left = sum(back_ref[b].astype(F32) for b in range(G)).astype(BF16)
    left_ref[...] = left
    right = sum(col_ref[a, 0:256, :].astype(F32) for a in range(G)).astype(BF16)
    right = tn(channel_major(), right).astype(BF16)
    right_ref[...] = right
    total = jnp.zeros((2 * C, F), F32)
    for i in range(RES):
        both = jnp.concatenate([left[i * C : i * C + C], right[i * C : i * C + C]], axis=0)
        total = total + nn(both, x_ref[i])
    rows = jnp.concatenate([total[:, 0:128], total[:, 128:256]], axis=0)
    half = pl.ds(pl.multiple_of(lax.axis_index("core") * 512, 512), 512)
    gout = gout_ref[half, :].astype(F32) + other_ref[half, :].astype(F32)
    for k in range(16):
        block = [gout[k * 32 : k * 32 + 32], rows[k * 8 : k * 8 + 8], jnp.zeros((8, 128), F32)]
        tail_ref[k] = jnp.concatenate(block, axis=0).astype(BF16)


def place():
    return lax.axis_index("zl") * 2 + lax.axis_index("yl")


def split_kernel(in_ref, update_ref, out_ref, *part_refs):
    sum_kernel(in_ref, out_ref)
    me = place()
    for k, ref in enumerate(part_refs):
        ref[...] = update_ref[lax.bitwise_xor(me, k)]


def join_kernel(in_ref, *refs):
    sum_kernel(in_ref, refs[G])
    me = place()
    for k in range(G):
        refs[G + 1][lax.bitwise_xor(me, k)] = refs[k][...]


def update_kernel(update_ref, out_ref):
    for b in range(G):
        part = update_ref[b].astype(F32)
        for i in range(RES):
            for a in range(G):
                at = i * 128 + a * 32 + b * 8
                out_ref[at : at + 8, :] = part[i * 32 + a * 8 : i * 32 + a * 8 + 8, :]


def msa_kernel(left_ref, right_ref, f1_ref, f2_ref, out_ref):
    factors = jnp.concatenate([f1_ref[...], f2_ref[...]], axis=0)
    for i in range(RES):
        both = jnp.concatenate([left_ref[i * C : i * C + C, :], right_ref[i * C : i * C + C, :]], axis=0)
        out_ref[i] = tn(both, factors).astype(BF16)


def sum_kernel(in_ref, out_ref):
    total = in_ref[0].astype(F32)
    for k in range(1, in_ref.shape[0]):
        total = total + in_ref[k].astype(F32)
    total = total.astype(BF16)
    for k in range(out_ref.shape[0]):
        out_ref[k] = total


def final_kernel(in_ref, gl_ref, gr_ref, gout_ref, wide):
    scale = 1.0 / 32
    rows = []
    for k in range(16):
        at = k // 4 * 8 + k % 4
        parts = [in_ref[at + core * 4].astype(F32) * scale for core in range(2)]
        for core in range(2):
            wide[(core * 16 + k) * 32 : (core * 16 + k) * 32 + 32, :] = parts[core][0:32]
        rows.append(parts[0][32:40] + parts[1][32:40])
    for h in range(2):
        for q, out in enumerate((gl_ref, gr_ref)):
            at = h * 8 + q * 4
            out[:, h * 128 : h * 128 + 128] = jnp.concatenate(rows[at : at + 4], axis=0)
    for c in range(C):
        gout_ref[c * 32 : c * 32 + 32, :] = wide[pl.ds(c, 32, stride=32), :]


def per_device(x, f1, f2, w, cot):
    x = x[0].reshape(S * RES, F)
    f1, f2 = f1.T, f2.T
    cot = cot[0].reshape(RES * 128, Z)
    row, x = call(
        pack_kernel,
        [shape((G, 512, S), BF16), shape((RES, S, F), BF16)],
        x,
        cot,
        scratch=[
            pltpu.VMEM((S * RES, F), BF16),
            pltpu.VMEM((RES * 128, Z), F32),
            pltpu.VMEM((2, S * RES + 8, 128), F32),
            pltpu.SemaphoreType.DMA((4,)),
        ],
        hbm=True,
        limit=210,
        flops=2 * 10**9,
    )
    row, right = call(
        project_kernel,
        [shape((G, 512, S), BF16), shape((256, S), BF16)],
        row,
        x,
        f1,
        f2,
        flops=33554432,
        aliases={0: 0},
    )
    row = exchange(row, ROW)
    col, grads, weight = call(
        right_kernel,
        [shape((G, 512, S), BF16), shape((1024, 1024), BF16), shape((128, 1024), BF16)],
        row,
        right,
        w,
        scratch=[pltpu.VMEM((1056, 128), F32)],
        flops=2 * 2 * 1024 * 1024 * 128,
    )
    col = exchange(col, COL)
    back, update, gout = call(
        left_kernel,
        [shape((G, 256, 128), BF16), shape((G, 256, 128), BF16), shape((1024, 128), BF16)],
        row,
        col,
        grads,
        weight,
        scratch=[pltpu.VMEM((1024, 1024), BF16)],
        flops=4 * 2 * 1024 * 1024 * 128,
    )
    other = lax.ppermute(gout, "core", [(0, 1), (1, 0)])
    back = exchange(back, ROW)
    left, right, tail = call(
        factor_kernel,
        [shape((256, S), BF16), shape((256, S), BF16), shape((16, 48, 128), BF16)],
        back,
        col,
        x,
        gout,
        other,
        flops=33554432,
    )
    (msa,) = call(msa_kernel, [shape((RES, S, F), BF16)], left, right, f1, f2, flops=33554432)
    tail = exchange(tail, NEAREST)
    tail, *updates = call(
        split_kernel, [shape((16, 48, 128), BF16)] + [shape((256, 128), BF16)] * G, tail, update
    )
    tail = exchange(tail, FAR)
    updates = [lax.ppermute(u, ROW, [(b, b ^ k) for b in range(G)]) if k else u for k, u in enumerate(updates)]
    tail, update = call(
        join_kernel, [shape((32, 48, 128), BF16), shape((G, 256, 128), BF16)], tail, *updates
    )
    (update,) = call(update_kernel, [shape((RES * 128, Z), F32)], update)
    tail = exchange(tail, NEAR)
    gl, gr, gout = call(
        final_kernel,
        [shape((C, F), F32), shape((C, F), F32), shape((1024, 128), F32)],
        tail,
        scratch=[pltpu.VMEM((1056, 128), F32)],
    )
    return update.reshape(1, RES, 128, Z), msa.transpose(1, 0, 2)[None], gl.T, gr.T, gout


def solution(mesh):
    split = Mesh(mesh.devices.reshape(4, 4, 2, 4, 2, 2), ("yh", "x", "core", "zh", "zl", "yl"))
    in_specs = (P(DP, None, AXIAL, None), P(), P(), P(), P(DP, AXIAL, None, None))
    out_specs = (P(DP, AXIAL, None, None), P(DP, None, AXIAL, None), P(), P(), P())
    return jax.shard_map(per_device, mesh=split, in_specs=in_specs, out_specs=out_specs, check_vma=False)
```

```python
import jax
import jax.numpy as jnp
from jax import lax
from jax.experimental import pallas as pl
from jax.experimental.pallas import tpu as pltpu
from jax.sharding import Mesh, PartitionSpec as P

BF16 = jnp.bfloat16
F32 = jnp.float32
ROW = ("zl", "yl")
COL = "zh"
NEAR = ("x", "core", "zl", "yl")
NEAREST = ("x", "zl", "yl")
FAR = ("zh", "yh")
AXIAL = ("zh", "zl", "yl")
DP = ("yh", "x", "core")

S = 128
RES = 8
C = 32
Z = 128
F = 256
G = 4


def dot(a, b, dims):
    return lax.dot_general(a, b, (dims, ((), ())), preferred_element_type=F32)


def nn(a, b):
    return dot(a, b, ((1,), (0,)))


def nt(a, b):
    return dot(a, b, ((1,), (1,)))


def tn(a, b):
    return dot(a, b, ((0,), (0,)))


def call(kernel, out, *args, scratch=(), flops=0, hbm=False, limit=96, aliases=None):
    size = sum(a.size * a.dtype.itemsize for a in args) + sum(
        o.size * o.dtype.itemsize for o in out
    )
    return pl.pallas_call(
        kernel,
        out_shape=out,
        in_specs=[pl.BlockSpec(memory_space=pltpu.HBM if hbm else pltpu.VMEM)] * len(args),
        out_specs=[pl.BlockSpec(memory_space=pltpu.VMEM)] * len(out),
        scratch_shapes=list(scratch),
        input_output_aliases=aliases or {},
        compiler_params=pltpu.CompilerParams(vmem_limit_bytes=limit * 1024 * 256),
        cost_estimate=pl.CostEstimate(flops=flops, bytes_accessed=size, transcendentals=0),
    )(*args)


def shape(dims, dtype):
    return jax.ShapeDtypeStruct(dims, dtype)


def partner(x, k):
    return lax.ppermute(x, ROW, [(b, b ^ k) for b in range(G)])


def exchange(x, axes):
    return lax.all_to_all(x, axes, split_axis=0, concat_axis=0, tiled=True)


def channel_major():
    n = RES * C
    p = lax.broadcasted_iota(jnp.int32, (n, n), 0)
    q = lax.broadcasted_iota(jnp.int32, (n, n), 1)
    same = ((p >> 3) == (q & 31)) & ((p & 7) == (q >> 5))
    return jnp.where(same, 1.0, 0.0).astype(BF16)


def pack_kernel(x_hbm, cot_hbm, row_ref, xt_ref, x_ref, cot_ref, wide, sems):
    loads = []
    for k in range(2):
        part = pl.ds(k * 512, 512)
        loads.append(pltpu.make_async_copy(x_hbm.at[part], x_ref.at[part], sems.at[k]))
    for k in range(2):
        part = pl.ds(k * 512, 512)
        loads.append(pltpu.make_async_copy(cot_hbm.at[part], cot_ref.at[part], sems.at[2 + k]))
    for load in loads:
        load.start()
    for k in range(2):
        loads[k].wait()
        for h in range(2):
            wide[h, k * 512 : k * 512 + 512, :] = x_ref[k * 512 : k * 512 + 512, h * 128 : h * 128 + 128].astype(F32)
        for i in range(RES):
            for h in range(2):
                xt_ref[i, k * 64 : k * 64 + 64, h * 128 : h * 128 + 128] = wide[
                    h, pl.ds(k * 512 + i, 64, stride=RES), :
                ].astype(BF16)
    for k in range(2):
        loads[2 + k].wait()
        for b in range(G):
            for i in range(k * 4, k * 4 + 4):
                for h in range(2):
                    at = i * 128 + h * 64 + b * 8
                    pair = jnp.concatenate([cot_ref[at : at + 8, :], cot_ref[at + 32 : at + 40, :]], axis=0)
                    row_ref[b, i * 32 + h * 16 : i * 32 + h * 16 + 16, :] = pair.astype(BF16)


def project_kernel(row_in, x_ref, f1_ref, f2_ref, row_ref, right_ref):
    del row_in
    factors = jnp.concatenate([f1_ref[...], f2_ref[...]], axis=0)
    left, right = [], []
    for i in range(RES):
        both = nt(factors, x_ref[i]).astype(BF16)
        left.append(both[:C])
        right.append(both[C:])
    left = jnp.concatenate(left, axis=0)
    for b in range(G):
        row_ref[b, 256:512, :] = left
    right_ref[...] = nn(channel_major(), jnp.concatenate(right, axis=0)).astype(BF16)


def swap_blocks(blocks):
    lane = lax.broadcasted_iota(jnp.int32, (32, 128), 1)
    low, even = (lane & 64) == 0, (lane & 32) == 0
    a, b, c, d = blocks
    a, c = jnp.where(low, a, pltpu.roll(c, 64, 1)), jnp.where(low, pltpu.roll(a, 64, 1), c)
    b, d = jnp.where(low, b, pltpu.roll(d, 64, 1)), jnp.where(low, pltpu.roll(b, 64, 1), d)
    a, b = jnp.where(even, a, pltpu.roll(b, 32, 1)), jnp.where(even, pltpu.roll(a, 96, 1), b)
    c, d = jnp.where(even, c, pltpu.roll(d, 32, 1)), jnp.where(even, pltpu.roll(c, 96, 1), d)
    return a, b, c, d


def right_kernel(row_ref, right_ref, w_ref, col_ref, grads_ref, weight_ref, wide):
    wide[0:1024, :] = w_ref[...].astype(F32)
    weight = jnp.concatenate([wide[pl.ds(e, 32, stride=32), :] for e in range(C)], axis=0)
    weight_ref[...] = weight.T.astype(BF16)
    weight = weight.astype(BF16)
    for b in range(G):
        for at in range(0, 1024, 128):
            grad = nt(weight[at : at + 128], row_ref[b, 0:256, :]).astype(BF16)
            for i in range(RES):
                grads_ref[b * 256 + i * 32 : b * 256 + i * 32 + 32, at : at + 128] = jnp.concatenate(
                    [grad[e * 32 : e * 32 + 32, i * 32 : i * 32 + 32] for e in range(4)], axis=1
                )
    lefts = jnp.concatenate([row_ref[b, 256:512, :] for b in range(G)], axis=0)
    rg = (tn(lefts, grads_ref[...]) * (1.0 / S)).T.reshape(C, G, RES, S)
    for a in range(G):
        col_ref[a, 0:256, :] = rg[:, a].reshape(C * RES, S).astype(BF16)
        col_ref[a, 256:512, :] = right_ref[...]


def left_kernel(row_ref, col_ref, grads_ref, weight_ref, out_ref, update_ref, gout_ref, outers):
    right = jnp.concatenate(
        [col_ref[a, 256:512, :].astype(F32).reshape(C, RES, S) for a in range(G)], axis=1
    ).reshape(C * G * RES, S).astype(BF16)
    for b in range(G):
        outer = (nt(row_ref[b, 256:512, :], right) * (1.0 / S)).astype(BF16)
        for i in range(0, 256, 128):
            for e in range(0, 1024, 128):
                blocks = [outer[i + q : i + q + 32, e : e + 128] for q in range(0, 128, 32)]
                for q, block in enumerate(swap_blocks(blocks)):
                    outers[e + q * 32 : e + q * 32 + 32, b * 256 + i : b * 256 + i + 128] = block
    for b in range(G):
        out_ref[b] = (nn(grads_ref[b * 256 : b * 256 + 256, :], right) * (1.0 / S)).astype(BF16)
    update = nn(weight_ref[...], outers[...])
    for b in range(G):
        update_ref[b] = update[:, b * 256 : b * 256 + 256].T.astype(BF16)
    cot = jnp.concatenate([row_ref[b, 0:256, :] for b in range(G)], axis=0)
    gout_ref[...] = nn(outers[...], cot).astype(BF16)


def factor_kernel(back_ref, col_ref, x_ref, gout_ref, other_ref, left_ref, right_ref, tail_ref):
    left = sum(back_ref[b].astype(F32) for b in range(G)).astype(BF16)
    left_ref[...] = left
    right = sum(col_ref[a, 0:256, :].astype(F32) for a in range(G)).astype(BF16)
    right = tn(channel_major(), right).astype(BF16)
    right_ref[...] = right
    total = jnp.zeros((2 * C, F), F32)
    for i in range(RES):
        both = jnp.concatenate([left[i * C : i * C + C], right[i * C : i * C + C]], axis=0)
        total = total + nn(both, x_ref[i])
    rows = jnp.concatenate([total[:, 0:128], total[:, 128:256]], axis=0)
    half = pl.ds(pl.multiple_of(lax.axis_index("core") * 512, 512), 512)
    gout = gout_ref[half, :].astype(F32) + other_ref[half, :].astype(F32)
    for k in range(16):
        block = [gout[k * 32 : k * 32 + 32], rows[k * 8 : k * 8 + 8], jnp.zeros((8, 128), F32)]
        tail_ref[k] = jnp.concatenate(block, axis=0).astype(BF16)


def place():
    return lax.axis_index("zl") * 2 + lax.axis_index("yl")


def split_kernel(in_ref, update_ref, out_ref, pair_ref):
    sum_kernel(in_ref, out_ref)
    me = place()
    pair_ref[0] = update_ref[lax.bitwise_xor(me, 2)]
    pair_ref[1] = update_ref[lax.bitwise_xor(me, 3)]


def join_kernel(in_ref, update_ref, got_ref, out_ref, own_ref, a_ref, pair_ref):
    sum_kernel(in_ref, out_ref)
    me = place()
    own_ref[...] = update_ref[me]
    a_ref[...] = got_ref[0]
    pair_ref[0] = update_ref[lax.bitwise_xor(me, 1)]
    pair_ref[1] = got_ref[1]


def update_kernel(own_ref, a_ref, pair_ref, out_ref):
    me = place()
    for k, block in enumerate((own_ref[...], pair_ref[0], a_ref[...], pair_ref[1])):
        b = lax.bitwise_xor(me, k)
        part = block.astype(F32)
        for i in range(RES):
            for a in range(G):
                at = pl.multiple_of(i * 128 + a * 32 + b * 8, 8)
                out_ref[pl.ds(at, 8), :] = part[i * 32 + a * 8 : i * 32 + a * 8 + 8, :]


def msa_kernel(left_ref, right_ref, f1_ref, f2_ref, out_ref):
    factors = jnp.concatenate([f1_ref[...], f2_ref[...]], axis=0)
    for i in range(RES):
        both = jnp.concatenate([left_ref[i * C : i * C + C, :], right_ref[i * C : i * C + C, :]], axis=0)
        out_ref[i] = tn(both, factors).astype(BF16)


def sum_kernel(in_ref, out_ref):
    total = in_ref[0].astype(F32)
    for k in range(1, in_ref.shape[0]):
        total = total + in_ref[k].astype(F32)
    total = total.astype(BF16)
    for k in range(out_ref.shape[0]):
        out_ref[k] = total


def final_kernel(in_ref, gl_ref, gr_ref, gout_ref, wide):
    scale = 1.0 / 32
    rows = []
    for k in range(16):
        at = k // 4 * 8 + k % 4
        parts = [in_ref[at + core * 4].astype(F32) * scale for core in range(2)]
        for core in range(2):
            wide[(core * 16 + k) * 32 : (core * 16 + k) * 32 + 32, :] = parts[core][0:32]
        rows.append(parts[0][32:40] + parts[1][32:40])
    for h in range(2):
        for q, out in enumerate((gl_ref, gr_ref)):
            at = h * 8 + q * 4
            out[:, h * 128 : h * 128 + 128] = jnp.concatenate(rows[at : at + 4], axis=0)
    for c in range(C):
        gout_ref[c * 32 : c * 32 + 32, :] = wide[pl.ds(c, 32, stride=32), :]


def per_device(x, f1, f2, w, cot):
    x = x[0].reshape(S * RES, F)
    f1, f2 = f1.T, f2.T
    cot = cot[0].reshape(RES * 128, Z)
    row, x = call(
        pack_kernel,
        [shape((G, 512, S), BF16), shape((RES, S, F), BF16)],
        x,
        cot,
        scratch=[
            pltpu.VMEM((S * RES, F), BF16),
            pltpu.VMEM((RES * 128, Z), F32),
            pltpu.VMEM((2, S * RES + 8, 128), F32),
            pltpu.SemaphoreType.DMA((4,)),
        ],
        hbm=True,
        limit=210,
        flops=2 * 10**9,
    )
    row, right = call(
        project_kernel,
        [shape((G, 512, S), BF16), shape((256, S), BF16)],
        row,
        x,
        f1,
        f2,
        flops=33554432,
        aliases={0: 0},
    )
    row = exchange(row, ROW)
    col, grads, weight = call(
        right_kernel,
        [shape((G, 512, S), BF16), shape((1024, 1024), BF16), shape((128, 1024), BF16)],
        row,
        right,
        w,
        scratch=[pltpu.VMEM((1056, 128), F32)],
        flops=2 * 2 * 1024 * 1024 * 128,
    )
    col = exchange(col, COL)
    back, update, gout = call(
        left_kernel,
        [shape((G, 256, 128), BF16), shape((G, 256, 128), BF16), shape((1024, 128), BF16)],
        row,
        col,
        grads,
        weight,
        scratch=[pltpu.VMEM((1024, 1024), BF16)],
        flops=4 * 2 * 1024 * 1024 * 128,
    )
    other = lax.ppermute(gout, "core", [(0, 1), (1, 0)])
    back = exchange(back, ROW)
    left, right, tail = call(
        factor_kernel,
        [shape((256, S), BF16), shape((256, S), BF16), shape((16, 48, 128), BF16)],
        back,
        col,
        x,
        gout,
        other,
        flops=33554432,
    )
    (msa,) = call(msa_kernel, [shape((RES, S, F), BF16)], left, right, f1, f2, flops=33554432)
    tail = exchange(tail, NEAREST)
    part, pair = shape((256, 128), BF16), shape((2, 256, 128), BF16)
    tail, first = call(split_kernel, [shape((16, 48, 128), BF16), pair], tail, update)
    tail = exchange(tail, FAR)
    tail, own, near, second = call(
        join_kernel, [shape((32, 48, 128), BF16), part, part, pair], tail, update, partner(first, 2)
    )
    (update,) = call(update_kernel, [shape((RES * 128, Z), F32)], own, near, partner(second, 1))
    tail = exchange(tail, NEAR)
    gl, gr, gout = call(
        final_kernel,
        [shape((C, F), F32), shape((C, F), F32), shape((1024, 128), F32)],
        tail,
        scratch=[pltpu.VMEM((1056, 128), F32)],
    )
    return update.reshape(1, RES, 128, Z), msa.transpose(1, 0, 2)[None], gl.T, gr.T, gout


def solution(mesh):
    split = Mesh(mesh.devices.reshape(4, 4, 2, 4, 2, 2), ("yh", "x", "core", "zh", "zl", "yl"))
    in_specs = (P(DP, None, AXIAL, None), P(), P(), P(), P(DP, AXIAL, None, None))
    out_specs = (P(DP, AXIAL, None, None), P(DP, None, AXIAL, None), P(), P(), P())
    return jax.shard_map(per_device, mesh=split, in_specs=in_specs, out_specs=out_specs, check_vma=False)
```

```python
import jax
import jax.numpy as jnp
from jax import lax
from jax.experimental import pallas as pl
from jax.experimental.pallas import tpu as pltpu
from jax.sharding import Mesh, PartitionSpec as P

BF16 = jnp.bfloat16
F32 = jnp.float32
ROW = ("zl", "yl")
COL = "zh"
NEAR = ("x", "core", "zl", "yl")
NEAREST = ("x", "zl", "yl")
FAR = ("zh", "yh")
AXIAL = ("zh", "zl", "yl")
DP = ("yh", "x", "core")

S = 128
RES = 8
C = 32
Z = 128
F = 256
G = 4


def dot(a, b, dims):
    return lax.dot_general(a, b, (dims, ((), ())), preferred_element_type=F32)


def nn(a, b):
    return dot(a, b, ((1,), (0,)))


def nt(a, b):
    return dot(a, b, ((1,), (1,)))


def tn(a, b):
    return dot(a, b, ((0,), (0,)))


def call(kernel, out, *args, scratch=(), flops=0, hbm=False, limit=96, aliases=None):
    size = sum(a.size * a.dtype.itemsize for a in args) + sum(
        o.size * o.dtype.itemsize for o in out
    )
    return pl.pallas_call(
        kernel,
        out_shape=out,
        in_specs=[pl.BlockSpec(memory_space=pltpu.HBM if hbm else pltpu.VMEM)] * len(args),
        out_specs=[pl.BlockSpec(memory_space=pltpu.VMEM)] * len(out),
        scratch_shapes=list(scratch),
        input_output_aliases=aliases or {},
        compiler_params=pltpu.CompilerParams(vmem_limit_bytes=limit * 1024 * 256),
        cost_estimate=pl.CostEstimate(flops=flops, bytes_accessed=size, transcendentals=0),
    )(*args)


def shape(dims, dtype):
    return jax.ShapeDtypeStruct(dims, dtype)


def partner(x, k):
    return lax.ppermute(x, ROW, [(b, b ^ k) for b in range(G)])


def exchange(x, axes):
    return lax.all_to_all(x, axes, split_axis=0, concat_axis=0, tiled=True)


def channel_major():
    n = RES * C
    p = lax.broadcasted_iota(jnp.int32, (n, n), 0)
    q = lax.broadcasted_iota(jnp.int32, (n, n), 1)
    same = ((p >> 3) == (q & 31)) & ((p & 7) == (q >> 5))
    return jnp.where(same, 1.0, 0.0).astype(BF16)


def pack_kernel(x_hbm, cot_hbm, row_ref, xt_ref, x_ref, cot_ref, wide, sems):
    loads = []
    for k in range(2):
        part = pl.ds(k * 512, 512)
        loads.append(pltpu.make_async_copy(x_hbm.at[part], x_ref.at[part], sems.at[k]))
    for k in range(2):
        part = pl.ds(k * 512, 512)
        loads.append(pltpu.make_async_copy(cot_hbm.at[part], cot_ref.at[part], sems.at[2 + k]))
    for load in loads:
        load.start()
    for k in range(2):
        loads[k].wait()
        for h in range(2):
            wide[h, k * 512 : k * 512 + 512, :] = x_ref[k * 512 : k * 512 + 512, h * 128 : h * 128 + 128].astype(F32)
        for i in range(RES):
            for h in range(2):
                xt_ref[i, k * 64 : k * 64 + 64, h * 128 : h * 128 + 128] = wide[
                    h, pl.ds(k * 512 + i, 64, stride=RES), :
                ].astype(BF16)
    for k in range(2):
        loads[2 + k].wait()
        for b in range(G):
            for i in range(k * 4, k * 4 + 4):
                for h in range(2):
                    at = i * 128 + h * 64 + b * 8
                    pair = jnp.concatenate([cot_ref[at : at + 8, :], cot_ref[at + 32 : at + 40, :]], axis=0)
                    row_ref[b, i * 32 + h * 16 : i * 32 + h * 16 + 16, :] = pair.astype(BF16)


def project_kernel(row_in, x_ref, f1_ref, f2_ref, row_ref, right_ref):
    del row_in
    factors = jnp.concatenate([f1_ref[...], f2_ref[...]], axis=0)
    left, right = [], []
    for i in range(RES):
        both = nt(factors, x_ref[i]).astype(BF16)
        left.append(both[:C])
        right.append(both[C:])
    left = jnp.concatenate(left, axis=0)
    for b in range(G):
        row_ref[b, 256:512, :] = left
    right_ref[...] = nn(channel_major(), jnp.concatenate(right, axis=0)).astype(BF16)


def swap_blocks(blocks):
    lane = lax.broadcasted_iota(jnp.int32, (32, 128), 1)
    low, even = (lane & 64) == 0, (lane & 32) == 0
    a, b, c, d = blocks
    a, c = jnp.where(low, a, pltpu.roll(c, 64, 1)), jnp.where(low, pltpu.roll(a, 64, 1), c)
    b, d = jnp.where(low, b, pltpu.roll(d, 64, 1)), jnp.where(low, pltpu.roll(b, 64, 1), d)
    a, b = jnp.where(even, a, pltpu.roll(b, 32, 1)), jnp.where(even, pltpu.roll(a, 96, 1), b)
    c, d = jnp.where(even, c, pltpu.roll(d, 32, 1)), jnp.where(even, pltpu.roll(c, 96, 1), d)
    return a, b, c, d


def right_kernel(row_ref, right_ref, w_ref, col_ref, grads_ref, weight_ref, wide):
    wide[0:1024, :] = w_ref[...].astype(F32)
    weight = jnp.concatenate([wide[pl.ds(e, 32, stride=32), :] for e in range(C)], axis=0)
    weight_ref[...] = weight.T.astype(BF16)
    weight = weight.astype(BF16)
    for b in range(G):
        for at in range(0, 1024, 128):
            grad = nt(weight[at : at + 128], row_ref[b, 0:256, :]).astype(BF16)
            for i in range(RES):
                grads_ref[b * 256 + i * 32 : b * 256 + i * 32 + 32, at : at + 128] = jnp.concatenate(
                    [grad[e * 32 : e * 32 + 32, i * 32 : i * 32 + 32] for e in range(4)], axis=1
                )
    lefts = jnp.concatenate([row_ref[b, 256:512, :] for b in range(G)], axis=0)
    rg = (tn(lefts, grads_ref[...]) * (1.0 / S)).T.reshape(C, G, RES, S)
    for a in range(G):
        col_ref[a, 0:256, :] = rg[:, a].reshape(C * RES, S).astype(BF16)
        col_ref[a, 256:512, :] = right_ref[...]


def left_kernel(row_ref, col_ref, grads_ref, weight_ref, out_ref, update_ref, gout_ref, outers):
    right = jnp.concatenate(
        [col_ref[a, 256:512, :].astype(F32).reshape(C, RES, S) for a in range(G)], axis=1
    ).reshape(C * G * RES, S).astype(BF16)
    for b in range(G):
        outer = (nt(row_ref[b, 256:512, :], right) * (1.0 / S)).astype(BF16)
        for i in range(0, 256, 128):
            for e in range(0, 1024, 128):
                blocks = [outer[i + q : i + q + 32, e : e + 128] for q in range(0, 128, 32)]
                for q, block in enumerate(swap_blocks(blocks)):
                    outers[e + q * 32 : e + q * 32 + 32, b * 256 + i : b * 256 + i + 128] = block
    for b in range(G):
        out_ref[b] = (nn(grads_ref[b * 256 : b * 256 + 256, :], right) * (1.0 / S)).astype(BF16)
    update = nn(weight_ref[...], outers[...])
    for b in range(G):
        update_ref[b] = update[:, b * 256 : b * 256 + 256].T.astype(BF16)
    cot = jnp.concatenate([row_ref[b, 0:256, :] for b in range(G)], axis=0)
    gout_ref[...] = nn(outers[...], cot).astype(BF16)


def factor_kernel(back_ref, col_ref, x_ref, gout_ref, other_ref, left_ref, right_ref, tail_ref):
    left = sum(back_ref[b].astype(F32) for b in range(G)).astype(BF16)
    left_ref[...] = left
    right = sum(col_ref[a, 0:256, :].astype(F32) for a in range(G)).astype(BF16)
    right = tn(channel_major(), right).astype(BF16)
    right_ref[...] = right
    total = jnp.zeros((2 * C, F), F32)
    for i in range(RES):
        both = jnp.concatenate([left[i * C : i * C + C], right[i * C : i * C + C]], axis=0)
        total = total + nn(both, x_ref[i])
    rows = jnp.concatenate([total[:, 0:128], total[:, 128:256]], axis=0)
    half = pl.ds(pl.multiple_of(lax.axis_index("core") * 512, 512), 512)
    gout = gout_ref[half, :].astype(F32) + other_ref[half, :].astype(F32)
    for k in range(16):
        block = [gout[k * 32 : k * 32 + 32], rows[k * 8 : k * 8 + 8], jnp.zeros((8, 128), F32)]
        tail_ref[k] = jnp.concatenate(block, axis=0).astype(BF16)


def place():
    return lax.axis_index("zl") * 2 + lax.axis_index("yl")


def split_kernel(in_ref, update_ref, out_ref, pair_ref):
    sum_kernel(in_ref, out_ref)
    me = place()
    pair_ref[0] = update_ref[lax.bitwise_xor(me, 2)]
    pair_ref[1] = update_ref[lax.bitwise_xor(me, 3)]


def join_kernel(in_ref, update_ref, got_ref, out_ref, own_ref, a_ref, pair_ref):
    sum_kernel(in_ref, out_ref)
    me = place()
    own_ref[...] = update_ref[me]
    a_ref[...] = got_ref[0]
    pair_ref[0] = update_ref[lax.bitwise_xor(me, 1)]
    pair_ref[1] = got_ref[1]


def update_kernel(own_ref, a_ref, pair_ref, after_ref, out_ref):
    del after_ref
    me = place()
    for k, block in enumerate((own_ref[...], pair_ref[0], a_ref[...], pair_ref[1])):
        b = lax.bitwise_xor(me, k)
        part = block.astype(F32)
        for i in range(RES):
            for a in range(G):
                at = pl.multiple_of(i * 128 + a * 32 + b * 8, 8)
                out_ref[pl.ds(at, 8), :] = part[i * 32 + a * 8 : i * 32 + a * 8 + 8, :]


def msa_kernel(left_ref, right_ref, f1_ref, f2_ref, out_ref):
    factors = jnp.concatenate([f1_ref[...], f2_ref[...]], axis=0)
    for i in range(RES):
        both = jnp.concatenate([left_ref[i * C : i * C + C, :], right_ref[i * C : i * C + C, :]], axis=0)
        out_ref[i] = tn(both, factors).astype(BF16)


def sum_kernel(in_ref, out_ref):
    total = in_ref[0].astype(F32)
    for k in range(1, in_ref.shape[0]):
        total = total + in_ref[k].astype(F32)
    total = total.astype(BF16)
    for k in range(out_ref.shape[0]):
        out_ref[k] = total


def final_kernel(in_ref, gl_ref, gr_ref, gout_ref, wide):
    scale = 1.0 / 32
    rows = []
    for k in range(16):
        at = k // 4 * 8 + k % 4
        parts = [in_ref[at + core * 4].astype(F32) * scale for core in range(2)]
        for core in range(2):
            wide[(core * 16 + k) * 32 : (core * 16 + k) * 32 + 32, :] = parts[core][0:32]
        rows.append(parts[0][32:40] + parts[1][32:40])
    for h in range(2):
        for q, out in enumerate((gl_ref, gr_ref)):
            at = h * 8 + q * 4
            out[:, h * 128 : h * 128 + 128] = jnp.concatenate(rows[at : at + 4], axis=0)
    for c in range(C):
        gout_ref[c * 32 : c * 32 + 32, :] = wide[pl.ds(c, 32, stride=32), :]


def per_device(x, f1, f2, w, cot):
    x = x[0].reshape(S * RES, F)
    f1, f2 = f1.T, f2.T
    cot = cot[0].reshape(RES * 128, Z)
    row, x = call(
        pack_kernel,
        [shape((G, 512, S), BF16), shape((RES, S, F), BF16)],
        x,
        cot,
        scratch=[
            pltpu.VMEM((S * RES, F), BF16),
            pltpu.VMEM((RES * 128, Z), F32),
            pltpu.VMEM((2, S * RES + 8, 128), F32),
            pltpu.SemaphoreType.DMA((4,)),
        ],
        hbm=True,
        limit=210,
        flops=2 * 10**9,
    )
    row, right = call(
        project_kernel,
        [shape((G, 512, S), BF16), shape((256, S), BF16)],
        row,
        x,
        f1,
        f2,
        flops=33554432,
        aliases={0: 0},
    )
    row = exchange(row, ROW)
    col, grads, weight = call(
        right_kernel,
        [shape((G, 512, S), BF16), shape((1024, 1024), BF16), shape((128, 1024), BF16)],
        row,
        right,
        w,
        scratch=[pltpu.VMEM((1056, 128), F32)],
        flops=2 * 2 * 1024 * 1024 * 128,
    )
    col = exchange(col, COL)
    back, update, gout = call(
        left_kernel,
        [shape((G, 256, 128), BF16), shape((G, 256, 128), BF16), shape((1024, 128), BF16)],
        row,
        col,
        grads,
        weight,
        scratch=[pltpu.VMEM((1024, 1024), BF16)],
        flops=4 * 2 * 1024 * 1024 * 128,
    )
    other = lax.ppermute(gout, "core", [(0, 1), (1, 0)])
    back = exchange(back, ROW)
    left, right, tail = call(
        factor_kernel,
        [shape((256, S), BF16), shape((256, S), BF16), shape((16, 48, 128), BF16)],
        back,
        col,
        x,
        gout,
        other,
        flops=33554432,
    )
    (msa,) = call(msa_kernel, [shape((RES, S, F), BF16)], left, right, f1, f2, flops=33554432)
    tail = exchange(tail, NEAREST)
    part, pair = shape((256, 128), BF16), shape((2, 256, 128), BF16)
    tail, first = call(split_kernel, [shape((16, 48, 128), BF16), pair], tail, update)
    tail = exchange(tail, FAR)
    tail, own, near, second = call(
        join_kernel, [shape((32, 48, 128), BF16), part, part, pair], tail, update, partner(first, 2)
    )
    tail = exchange(tail, NEAR)
    gl, gr, gout = call(
        final_kernel,
        [shape((C, F), F32), shape((C, F), F32), shape((1024, 128), F32)],
        tail,
        scratch=[pltpu.VMEM((1056, 128), F32)],
    )
    (update,) = call(update_kernel, [shape((RES * 128, Z), F32)], own, near, partner(second, 1), gl)
    return update.reshape(1, RES, 128, Z), msa.transpose(1, 0, 2)[None], gl.T, gr.T, gout


def solution(mesh):
    split = Mesh(mesh.devices.reshape(4, 4, 2, 4, 2, 2), ("yh", "x", "core", "zh", "zl", "yl"))
    in_specs = (P(DP, None, AXIAL, None), P(), P(), P(), P(DP, AXIAL, None, None))
    out_specs = (P(DP, AXIAL, None, None), P(DP, None, AXIAL, None), P(), P(), P())
    return jax.shard_map(per_device, mesh=split, in_specs=in_specs, out_specs=out_specs, check_vma=False)
```
